32 devices in a mesh: row: 8 (over z, core), col: 4 (over y, x).
Axes of the slice: x: 2, y: 2, z: 4, core: 2. Of those that a mesh axis runs over, the one named last changes fastest.
Arguments:
- occ_irrep: int32 [128], replicated, may hold values from 0 to 7
- vir_irrep: int32 [1024], replicated, may hold values from 0 to 7
- w_slab: bfloat16 [3072, 131072], P('row', 'col'), may hold values from -0.046875 to 0.046875
- amplitudes: bfloat16 [256, 131072], P('row', 'col'), may hold values from -6 to 6
Outputs:
- cycle_term: float32 [256, 3072], P('col', 'row')
The draws below stay inside these ranges and needn't reach their ends.
Inputs may be any that keep to these rules, and one draw needn't show every extreme that they name: `occ_irrep`: D2h irrep labels. `vir_irrep`: D2h irrep labels.
All inputs are finite; a program needn't handle non-finite values.
Results may differ from the reference program's by a relative error of at most 0.0003.
Values may be sent and summed in bfloat16 or wider, within the bound.
A program may use at most 128 MiB of HBM per device.

```python
import jax
import jax.numpy as jnp
from jax import lax

NOCC = 128
NVIR = 1024
NCOL = 256
KORD = 131072
ROWS = 3072
N_COL = 4


def touch_ends(drawn, own_key, smallest, high):
    longest = drawn.shape.index(max(drawn.shape))
    spots = []
    for shift in (0, 1):
        where = [jax.random.randint(jax.random.fold_in(own_key, axis), (), 0, length) for axis, length in enumerate(drawn.shape)]
        where[longest] = (where[longest] + shift) % drawn.shape[longest]
        spots.append(tuple(where))
    return drawn.at[spots[0]].set(smallest).at[spots[1]].set(high)


def raised(entries, key, source, target, parts, factor):
    owner, partner = [(jnp.arange(entries.shape[dim]) // (entries.shape[dim] // parts)).reshape([-1 if axis == dim else 1 for axis in range(entries.ndim)]) for dim in (source, target)]
    chosen = jax.random.permutation(key, parts)[partner]
    strong = (owner == chosen) | (owner == (partner + parts // 2) % parts)
    return jnp.where(strong, factor * entries, entries)


def steps_of(own_key, dims, cuts, smallest, top_value):
    level, own = 1.0, jax.random.fold_in(own_key, 6)
    for dim, shards_of in cuts:
        steps = jnp.exp(jax.random.uniform(jax.random.fold_in(own, dim), (shards_of,), jnp.float32, smallest / len(cuts), top_value / len(cuts)))
        level = level * jnp.repeat(steps, dims[dim] // shards_of).reshape([-1 if axis == dim else 1 for axis in range(len(dims))])
    return level


def normal_values(rng, extent, spread, reach, shards=(), kind=jnp.bfloat16):
    factor_of = steps_of(rng, extent, shards, -0.22, 0.18) if shards else 1.0
    array = jax.random.normal(rng, extent, jnp.float32) * spread * factor_of
    return jnp.minimum(jnp.maximum(array, -reach), reach).astype(kind)


def heavy_noise(stream_key, extent, spread, limit, cuts, heavy, kind=jnp.bfloat16):
    values = spread * jax.random.normal(stream_key, extent, jnp.float32)
    if cuts:
        values = values * steps_of(stream_key, extent, cuts, -0.22, 0.18)
    return jnp.clip(raised(values, jax.random.fold_in(stream_key, 3), *heavy), -limit, limit).astype(kind)


def setup_inputs(seed: int = 0) -> dict:
    streams_of = jax.random.split(jax.random.key(seed), 5)
    occ_irrep = touch_ends(jax.random.randint(streams_of[0], (NOCC,), 0, 8), jax.random.fold_in(streams_of[0], 1), 0, 7).astype(jnp.int32)
    vir_irrep = touch_ends(jax.random.randint(streams_of[1], (NVIR,), 0, 8), jax.random.fold_in(streams_of[1], 1), 0, 7).astype(jnp.int32)
    w_slab = normal_values(streams_of[2], (ROWS, KORD), (KORD // 8) ** -0.5, 0.046875, ((0, 8), (1, 4)))
    amplitudes = heavy_noise(streams_of[3], (NCOL, KORD), 1.0, 6.0, ((0, 8), (1, 4)), (1, 0, 8, 2.0))
    return {"occ_irrep": occ_irrep, "vir_irrep": vir_irrep, "w_slab": w_slab, "amplitudes": amplitudes}


def labels(index, occ_irrep, vir_irrep):
    nvir = vir_irrep.shape[0]
    occ_part = jnp.take(occ_irrep, index // nvir)
    vir_part = jnp.take(vir_irrep, index % nvir)
    return jnp.bitwise_xor(occ_part, vir_part)


def reference(occ_irrep, vir_irrep, w_slab, amplitudes):
    nrows = w_slab.shape[0]
    korder = w_slab.shape[1]
    ncols = amplitudes.shape[0]
    block = korder // N_COL
    row_labels = labels(jnp.arange(nrows, dtype=jnp.int32), occ_irrep, vir_irrep)

    def accumulate(total, step):
        start = (step * block).astype(jnp.int32)
        w_block = lax.dynamic_slice_in_dim(w_slab, start, block, 1)
        a_block = lax.dynamic_slice_in_dim(amplitudes, start, block, 1)
        col_labels = labels(start + jnp.arange(block, dtype=jnp.int32), occ_irrep, vir_irrep)
        keep = row_labels[:, None] == col_labels[None, :]
        masked = jnp.where(keep, w_block, jnp.zeros_like(w_block))
        total = total + jnp.dot(a_block, masked.T, preferred_element_type=jnp.float32)
        return total, None

    start_total = jnp.zeros((ncols, nrows), jnp.float32)
    result, _ = lax.scan(accumulate, start_total, jnp.arange(N_COL, dtype=jnp.int32))
    return result
```

```python
import functools

import jax
import jax.numpy as jnp
from jax import lax
from jax.experimental import pallas as pl
from jax.experimental.pallas import tpu as pltpu
from jax.sharding import PartitionSpec as P
from math import gcd

MESH = pl.DeviceIdType.MESH
NT = (((1,), (1,)), ((), ()))


def kernel(nrow, ncol, kc, occ_ref, vir_row, vir_col, w_hbm, a_hbm, out_ref,
           gath, wm, acc, red, w_sem, own_sem, send_sem, recv_sem, rs_send, rs_recv):
    rho = lax.axis_index("row")
    kap = lax.axis_index("col")
    chips = nrow // 2
    chip = rho // 2
    core = rho % 2
    other = chip * 2 + 1 - core
    rows, depth = a_hbm.shape
    nr = w_hbm.shape[0]
    nvir = vir_row.shape[1]
    nq = depth // kc
    per_q = kc // nvir
    spo = nrow // ncol
    sub = gcd(nr, nvir)
    has_up = chip < chips - 1
    has_down = chip > 0

    def w_copy(j):
        cols = pl.ds(pl.multiple_of(j * nvir, nvir), nvir)
        return pltpu.make_async_copy(w_hbm.at[:, cols], wm.at[:, cols], w_sem.at[j])

    def chunk(q):
        return pl.ds(pl.multiple_of(q * kc, kc), kc)

    def own_copy(q):
        return pltpu.make_async_copy(a_hbm.at[:, chunk(q)], gath.at[rho, :, chunk(q)], own_sem.at[q])

    def remote(way, s, q, own=False):
        target = (rho + 2, rho - 2, other)[way]
        src = a_hbm.at[:, chunk(q)] if own else gath.at[s, :, chunk(q)]
        return pltpu.make_async_remote_copy(
            src_ref=src, dst_ref=gath.at[s, :, chunk(q)],
            send_sem=send_sem.at[way, s, q], recv_sem=recv_sem.at[s, q],
            device_id=(target, kap), device_id_type=MESH)

    def reduce_copy(s):
        return pltpu.make_async_remote_copy(
            src_ref=acc.at[s], dst_ref=red.at[kap, s % spo],
            send_sem=rs_send.at[s], recv_sem=rs_recv.at[kap, s % spo],
            device_id=(rho, s // spo), device_id_type=MESH)

    def loop(n, f):
        def step(i, c):
            f(i)
            return c
        lax.fori_loop(0, n, step, 0)

    loop(nq, lambda q: own_copy(q).start())
    loop(nq * per_q, lambda j: w_copy(j).start())

    barrier = pltpu.get_barrier_semaphore()

    @pl.when(has_up)
    def _():
        pl.semaphore_signal(barrier, inc=1, device_id=(rho + 2, kap), device_id_type=MESH)

    @pl.when(has_down)
    def _():
        pl.semaphore_signal(barrier, inc=1, device_id=(rho - 2, kap), device_id_type=MESH)

    pl.semaphore_signal(barrier, inc=1, device_id=(other, kap), device_id_type=MESH)
    for t in range(1, ncol):
        pl.semaphore_signal(barrier, inc=1, device_id=(rho, lax.rem(kap + t, ncol)), device_id_type=MESH)
    pl.semaphore_wait(barrier, ncol + has_up.astype(jnp.int32) + has_down.astype(jnp.int32))

    def send_own(q):
        @pl.when(has_up)
        def _():
            remote(0, rho, q, True).start()

        @pl.when(has_down)
        def _():
            remote(1, rho, q, True).start()

        remote(2, rho, q, True).start()

    loop(nq, send_own)
    acc[...] = jnp.zeros_like(acc)

    def mask(j):
        w_copy(j).wait()
        cols = pl.ds(pl.multiple_of(j * nvir, nvir), nvir)
        col_labels = vir_row[...] ^ occ_ref[kap * (depth // nvir) + j]
        for b in range(nr // sub):
            start = rho * nr + b * sub
            at = pl.multiple_of(lax.rem(start, nvir), sub)
            row_labels = vir_col[pl.ds(at, sub), :] ^ occ_ref[start // nvir]
            block = wm[b * sub:(b + 1) * sub, cols].astype(jnp.float32)
            kept = jnp.where(row_labels == col_labels, block, 0.0)
            wm[b * sub:(b + 1) * sub, cols] = kept.astype(wm.dtype)

    def product(p, q):
        a = gath[pl.ds(2 * p, 2), :, chunk(q)].reshape(2 * rows, kc)
        part = lax.dot_general(a, wm[:, chunk(q)], NT, preferred_element_type=jnp.float32)
        acc[pl.ds(2 * p, 2)] += part.reshape(2, rows, nr)

    def finish(p):
        for e in range(2):
            s = 2 * p + e

            @pl.when(s // spo != kap)
            def _():
                reduce_copy(s).start()

    def own_step(q):
        loop(per_q, lambda j: mask(q * per_q + j))
        own_copy(q).wait()
        remote(2, other, q).wait_recv()
        product(chip, q)

    loop(nq, own_step)
    finish(chip)

    def far_step(i):
        d = i // nq + 1
        q = i % nq
        for way in range(2):
            p = chip - d if way == 0 else chip + d
            there = p >= 0 if way == 0 else p < chips
            onward = has_up if way == 0 else has_down

            @pl.when(there)
            def _():
                s = 2 * p + core
                remote(way, s, q).wait_recv()

                @pl.when(onward)
                def _():
                    remote(way, s, q).start()

                remote(2, s, q).start()

        for way in range(2):
            p = chip - d if way == 0 else chip + d
            there = p >= 0 if way == 0 else p < chips

            @pl.when(there)
            def _():
                remote(2, 2 * p + 1 - core, q).wait_recv()
                product(p, q)

                @pl.when(q == nq - 1)
                def _():
                    finish(p)

    loop((chips - 1) * nq, far_step)

    for i in range(spo):
        total = acc[kap * spo + i]
        for t in range(1, ncol):
            peer = lax.rem(kap + t, ncol)
            pltpu.make_async_remote_copy(
                src_ref=acc.at[i], dst_ref=red.at[peer, i],
                send_sem=rs_send.at[i], recv_sem=rs_recv.at[peer, i],
                device_id=(rho, peer), device_id_type=MESH).wait_recv()
            total = total + red[peer, i]
        out_ref[i * rows:(i + 1) * rows, :] = total

    def drain(i):
        p = i // nq
        q = i % nq
        s = 2 * p + core

        @pl.when(has_up & (p <= chip))
        def _():
            remote(0, s, q).wait_send()

        @pl.when(has_down & (p >= chip))
        def _():
            remote(1, s, q).wait_send()

        remote(2, s, q).wait_send()

    loop(chips * nq, drain)

    def drain_reduce(s):
        @pl.when(s // spo != kap)
        def _():
            reduce_copy(s).wait_send()

    loop(nrow, drain_reduce)


def body(nrow, ncol, occ_irrep, vir_irrep, w_slab, amplitudes):
    rows, depth = amplitudes.shape
    nr = w_slab.shape[0]
    nvir = vir_irrep.shape[0]
    kc = 4096 if depth % 4096 == 0 else depth
    nq = depth // kc
    spo = nrow // ncol
    vmem = pl.BlockSpec(memory_space=pltpu.VMEM)
    anywhere = pl.BlockSpec(memory_space=pl.ANY)
    return pl.pallas_call(
        functools.partial(kernel, nrow, ncol, kc),
        out_shape=jax.ShapeDtypeStruct((spo * rows, nr), jnp.float32),
        in_specs=[pl.BlockSpec(memory_space=pltpu.SMEM), vmem, vmem, anywhere, anywhere],
        out_specs=vmem,
        scratch_shapes=[
            pltpu.VMEM((nrow, rows, depth), amplitudes.dtype),
            pltpu.VMEM((nr, depth), w_slab.dtype),
            pltpu.VMEM((nrow, rows, nr), jnp.float32),
            pltpu.VMEM((ncol, spo, rows, nr), jnp.float32),
            pltpu.SemaphoreType.DMA((depth // nvir,)),
            pltpu.SemaphoreType.DMA((nq,)),
            pltpu.SemaphoreType.DMA((3, nrow, nq)),
            pltpu.SemaphoreType.DMA((nrow, nq)),
            pltpu.SemaphoreType.DMA((nrow,)),
            pltpu.SemaphoreType.DMA((ncol, spo)),
        ],
        compiler_params=pltpu.CompilerParams(
            collective_id=0, has_side_effects=True, vmem_limit_bytes=56 * 1024 * 1024),
        cost_estimate=pl.CostEstimate(
            flops=2 * nrow * rows * nr * depth, bytes_accessed=2 * nr * depth, transcendentals=0),
    )(occ_irrep, vir_irrep.reshape(1, nvir), vir_irrep.reshape(nvir, 1), w_slab, amplitudes)


def solution(mesh):
    placed = (P(), P(), P("row", "col"), P("row", "col"))
    shape = dict(mesh.shape)
    return jax.shard_map(
        functools.partial(body, shape["row"], shape["col"]), mesh=mesh,
        in_specs=placed, out_specs=P("col", "row"), check_vma=False)
```

```python
import functools

import jax
import jax.numpy as jnp
from jax import lax
from jax.experimental import pallas as pl
from jax.experimental.pallas import tpu as pltpu
from jax.sharding import PartitionSpec as P
from math import gcd

MESH = pl.DeviceIdType.MESH
NT = (((1,), (1,)), ((), ()))
KC = 2048


def kernel(nrow, ncol, kc, nh, cap, occ_ref, vir_row, w_hbm, a_hbm, out_ref,
           gath, wm, acc, red, row_lab, w_sem, own_sem, send_sem, recv_sem, rs_send, rs_recv,
           v_out=None, v_in=None, w_help=None, p_out=None, p_in=None, help_lab=None,
           spread=None, fold=None, v_send=None, v_recv=None, p_send=None, p_recv=None):
    rho = lax.axis_index("row")
    kap = lax.axis_index("col")
    chips = nrow // 2
    chip = rho // 2
    core = rho % 2
    other = chip * 2 + 1 - core
    rows, depth = a_hbm.shape
    nr = w_hbm.shape[0]
    nvir = vir_row.shape[1]
    nq = depth // kc
    per_q = kc // nvir
    spo = nrow // ncol
    sub = gcd(nr, nvir)
    has_up = chip < chips - 1
    has_down = chip > 0
    if nh:
        first, last = chip == 0, chip == chips - 1
        is_end = first | last
        below, above = chip == 1, chip == chips - 2
        helper = below | above
        up_from = jnp.where(above, nh, 0)
        down_from = jnp.where(below, nh, 0)
        lead = nq - 2 * nh
        helped = jnp.where(below, rho - 2, rho + 2)
        end_chip = jnp.where(below, 0, chips - 1)
        patron = jnp.where(first, rho + 2, rho - 2)
    else:
        up_from = down_from = 0

    def w_copy(j):
        cols = pl.ds(pl.multiple_of(j * nvir, nvir), nvir)
        return pltpu.make_async_copy(w_hbm.at[:, cols], wm.at[:, cols], w_sem.at[j])

    def chunk(q):
        return pl.ds(pl.multiple_of(q * kc, kc), kc)

    def own_copy(q):
        return pltpu.make_async_copy(a_hbm.at[:, chunk(q)], gath.at[rho, :, chunk(q)], own_sem.at[q])

    def remote(way, s, q, own=False):
        target = (rho + 2, rho - 2, other)[way]
        src = a_hbm.at[:, chunk(q)] if own else gath.at[s, :, chunk(q)]
        return pltpu.make_async_remote_copy(
            src_ref=src, dst_ref=gath.at[s, :, chunk(q)],
            send_sem=send_sem.at[way, s, q], recv_sem=recv_sem.at[s, q],
            device_id=(target, kap), device_id_type=MESH)

    def reduce_copy(s):
        return pltpu.make_async_remote_copy(
            src_ref=acc.at[s], dst_ref=red.at[kap, s % spo],
            send_sem=rs_send.at[s], recv_sem=rs_recv.at[kap, s % spo],
            device_id=(rho, s // spo), device_id_type=MESH)

    def loop(n, f):
        def step(i, c):
            f(i)
            return c
        lax.fori_loop(0, n, step, 0)

    loop(nq, lambda q: own_copy(q).start())
    loop(nq * per_q, lambda j: w_copy(j).start())

    barrier = pltpu.get_barrier_semaphore()

    @pl.when(has_up)
    def _():
        pl.semaphore_signal(barrier, inc=1, device_id=(rho + 2, kap), device_id_type=MESH)

    @pl.when(has_down)
    def _():
        pl.semaphore_signal(barrier, inc=1, device_id=(rho - 2, kap), device_id_type=MESH)

    pl.semaphore_signal(barrier, inc=1, device_id=(other, kap), device_id_type=MESH)
    for t in range(1, ncol):
        pl.semaphore_signal(barrier, inc=1, device_id=(rho, lax.rem(kap + t, ncol)), device_id_type=MESH)
    pl.semaphore_wait(barrier, ncol + has_up.astype(jnp.int32) + has_down.astype(jnp.int32))

    def send_far(q):
        @pl.when(has_up & (q >= up_from))
        def _():
            remote(0, rho, q, True).start()

        @pl.when(has_down & (q >= down_from))
        def _():
            remote(1, rho, q, True).start()

    def send_own(q):
        remote(2, rho, q, True).start()
        if nh:
            @pl.when((q < lead) | jnp.logical_not(is_end))
            def _():
                send_far(q)
        else:
            send_far(q)

    loop(nq, send_own)
    acc[...] = jnp.zeros_like(acc)

    def lane_labels(owner, b):
        start = owner * nr + b * sub
        at = pl.multiple_of(lax.rem(start, nvir), sub)
        return (vir_row[:, pl.ds(at, sub)] ^ occ_ref[start // nvir]).astype(jnp.float32)

    sub_i = lax.broadcasted_iota(jnp.int32, (sub, sub), 0)
    lane_i = lax.broadcasted_iota(jnp.int32, (sub, sub), 1)

    def write_labels(owner, ref):
        for b in range(nr // sub):
            wide = jnp.broadcast_to(lane_labels(owner, b), (sub, sub))
            ref[b * sub:(b + 1) * sub, :] = jnp.sum(
                jnp.where(sub_i == lane_i, wide, 0.0), axis=1, keepdims=True)

    def col_labels(j):
        return (vir_row[...] ^ occ_ref[kap * (depth // nvir) + j]).astype(jnp.float32)

    write_labels(rho, row_lab)

    def mask(j):
        w_copy(j).wait()
        cols = pl.ds(pl.multiple_of(j * nvir, nvir), nvir)
        labels = col_labels(j)
        for b in range(nr // sub):
            block = wm[b * sub:(b + 1) * sub, cols].astype(jnp.float32)
            kept = jnp.where(row_lab[b * sub:(b + 1) * sub, :] == labels, block, 0.0)
            wm[b * sub:(b + 1) * sub, cols] = kept.astype(wm.dtype)

    if nh:
        def v_copy(g):
            return pltpu.make_async_remote_copy(
                src_ref=v_out.at[g], dst_ref=v_in.at[g],
                send_sem=v_send.at[g], recv_sem=v_recv.at[g],
                device_id=(patron, kap), device_id_type=MESH)

        def p_copy(p):
            at = pl.ds(2 * p, 2)
            return pltpu.make_async_remote_copy(
                src_ref=p_out.at[at], dst_ref=p_in.at[at],
                send_sem=p_send.at[p], recv_sem=p_recv.at[p],
                device_id=(helped, kap), device_id_type=MESH)

        @pl.when(is_end)
        def _():
            for b in range(nr // sub):
                mine = lane_labels(rho, b)
                rank = jnp.zeros((1, sub), jnp.float32)
                for c in range(b + 1):
                    same = row_lab[c * sub:(c + 1) * sub, :] == mine
                    if c == b:
                        same = same & (sub_i < lane_i)
                    rank = rank + jnp.sum(jnp.where(same, 1.0, 0.0), axis=0, keepdims=True)
                slot = lax.broadcasted_iota(jnp.int32, (cap, sub), 0).astype(jnp.float32)
                fold[:, b * sub:(b + 1) * sub] = jnp.where(slot == rank, 1.0, 0.0).astype(fold.dtype)

        @pl.when(helper)
        def _():
            p_out[...] = jnp.zeros_like(p_out)
            write_labels(helped, help_lab)
            for b in range(nr // sub):
                mine = help_lab[b * sub:(b + 1) * sub, :]
                rank = jnp.zeros((sub, 1), jnp.float32)
                for c in range(b + 1):
                    same = mine == lane_labels(helped, c)
                    if c == b:
                        same = same & (lane_i < sub_i)
                    rank = rank + jnp.sum(jnp.where(same, 1.0, 0.0), axis=1, keepdims=True)
                slot = lax.broadcasted_iota(jnp.int32, (sub, cap), 1).astype(jnp.float32)
                spread[b * sub:(b + 1) * sub, :] = jnp.where(slot == rank, 1.0, 0.0).astype(spread.dtype)

        def send_folded(g):
            def part(j):
                at = pl.ds(pl.multiple_of(j * nvir, nvir), nvir)
                cols = pl.ds(pl.multiple_of(g * kc + j * nvir, nvir), nvir)
                v = jnp.dot(fold[...], wm[:, cols], preferred_element_type=jnp.float32)
                v_out[g, :, at] = v.astype(v_out.dtype)

            loop(per_q, part)
            v_copy(g).start()
            send_far(lead + 2 * g)
            send_far(lead + 2 * g + 1)

        def help_with(g):
            v_copy(g).wait_recv()

            def part(j):
                at = pl.ds(pl.multiple_of(j * nvir, nvir), nvir)
                labels = col_labels(g * per_q + j)
                for b in range(nr // sub):
                    rows_b = slice(b * sub, (b + 1) * sub)
                    block = jnp.dot(spread[rows_b, :], v_in[g, :, at], preferred_element_type=jnp.float32)
                    kept = jnp.where(help_lab[rows_b, :] == labels, block, 0.0)
                    w_help[rows_b, at] = kept.astype(w_help.dtype)

            loop(per_q, part)

            def one(t):
                p = jnp.where(below, t + 1, t)
                a = gath[pl.ds(2 * p, 2), :, chunk(g)].reshape(2 * rows, kc)
                p_part = lax.dot_general(a, w_help[...], NT, preferred_element_type=jnp.float32)
                p_out[pl.ds(2 * p, 2)] += p_part.reshape(2, rows, nr)

                @pl.when(g == nh - 1)
                def _():
                    p_copy(p).start()

            loop(chips - 1, one)

    def product(p, q):
        a = gath[pl.ds(2 * p, 2), :, chunk(q)].reshape(2 * rows, kc)
        part = lax.dot_general(a, wm[:, chunk(q)], NT, preferred_element_type=jnp.float32)
        acc[pl.ds(2 * p, 2)] += part.reshape(2, rows, nr)

    def finish(p):
        for e in range(2):
            s = 2 * p + e

            @pl.when(s // spo != kap)
            def _():
                reduce_copy(s).start()

    def own_step(q):
        loop(per_q, lambda j: mask(q * per_q + j))
        if nh:
            @pl.when(is_end & (q < nh))
            def _():
                send_folded(q)

        own_copy(q).wait()
        remote(2, other, q).wait_recv()
        product(chip, q)

    loop(nq, own_step)
    finish(chip)

    def source(way, i):
        d = i // nq + 1
        q = i % nq
        p = chip - d if way == 0 else chip + d
        there = p >= 0 if way == 0 else p < chips
        if nh:
            there = there & jnp.logical_not(is_end & (q < nh))
            slow = below if way == 0 else above
            j = jnp.maximum(i - lead + 2, 0)
            g = (2 * j + 1) // 9
            off = j - (9 * g) // 2
            early = i < lead
            later = (i >= lead) & (g >= 1) & (g <= nh) & (off >= 1) & (off <= 2)
            slow_q = jnp.where(early, i, jnp.where(later, lead + 2 * (g - 1) + off - 1, 0))
            p = jnp.where(slow, end_chip, p)
            q = jnp.where(slow, slow_q, q)
            there = (slow & (early | later)) | (jnp.logical_not(slow) & there)
        return p, q, there

    def far_step(i):
        for way in range(2):
            p, q, there = source(way, i)
            onward = has_up & (q >= up_from) if way == 0 else has_down & (q >= down_from)

            @pl.when(there)
            def _():
                s = 2 * p + core
                remote(way, s, q).wait_recv()

                @pl.when(onward)
                def _():
                    remote(way, s, q).start()

                remote(2, s, q).start()

        for way in range(2):
            p, q, there = source(way, i)

            @pl.when(there)
            def _():
                remote(2, 2 * p + 1 - core, q).wait_recv()
                product(p, q)

                @pl.when((q == nq - 1) & jnp.logical_not(is_end) if nh else q == nq - 1)
                def _():
                    finish(p)

        if nh:
            def maybe(g):
                ready = jnp.maximum(lead - 2 + (9 * (g + 1)) // 2, (chips - 3) * nq + g)

                @pl.when(i == ready)
                def _():
                    help_with(g)

            @pl.when(helper)
            def _():
                loop(nh, maybe)

    loop((chips - 1) * nq, far_step)

    if nh:
        @pl.when(is_end)
        def _():
            def settle(t):
                p = jnp.where(first, t + 1, chips - 2 - t)
                at = pl.ds(2 * p, 2)
                pltpu.make_async_remote_copy(
                    src_ref=p_out.at[at], dst_ref=p_in.at[at],
                    send_sem=p_send.at[p], recv_sem=p_recv.at[p],
                    device_id=(patron, kap), device_id_type=MESH).wait_recv()
                acc[at] += p_in[at]
                finish(p)

            loop(chips - 1, settle)

    for i in range(spo):
        total = acc[kap * spo + i]
        for t in range(1, ncol):
            peer = lax.rem(kap + t, ncol)
            pltpu.make_async_remote_copy(
                src_ref=acc.at[i], dst_ref=red.at[peer, i],
                send_sem=rs_send.at[i], recv_sem=rs_recv.at[peer, i],
                device_id=(rho, peer), device_id_type=MESH).wait_recv()
            total = total + red[peer, i]
        out_ref[i * rows:(i + 1) * rows, :] = total

    def drain(i):
        p = i // nq
        q = i % nq
        s = 2 * p + core

        @pl.when(has_up & (p <= chip) & (q >= up_from))
        def _():
            remote(0, s, q).wait_send()

        @pl.when(has_down & (p >= chip) & (q >= down_from))
        def _():
            remote(1, s, q).wait_send()

        @pl.when((p == chip) | jnp.logical_not(is_end & (q < nh)) if nh else p >= 0)
        def _():
            remote(2, s, q).wait_send()

    loop(chips * nq, drain)

    if nh:
        @pl.when(is_end)
        def _():
            loop(nh, lambda g: v_copy(g).wait_send())

        @pl.when(helper)
        def _():
            loop(chips - 1, lambda t: p_copy(jnp.where(below, t + 1, t)).wait_send())

    def drain_reduce(s):
        @pl.when(s // spo != kap)
        def _():
            reduce_copy(s).wait_send()

    loop(nrow, drain_reduce)


def body(nrow, ncol, occ_irrep, vir_irrep, w_slab, amplitudes):
    rows, depth = amplitudes.shape
    nr = w_slab.shape[0]
    nvir = vir_irrep.shape[0]
    kc = KC if depth % KC == 0 else depth
    nq = depth // kc
    spo = nrow // ncol
    cap = -(-nr * 5 // 24 // 16) * 16
    help_chunks = 3 * nq // 8 if nrow // 2 >= 4 else 0
    vmem = pl.BlockSpec(memory_space=pltpu.VMEM)
    anywhere = pl.BlockSpec(memory_space=pl.ANY)

    def call(nh, *args):
        scratch = [
            pltpu.VMEM((nrow, rows, depth), amplitudes.dtype),
            pltpu.VMEM((nr, depth), w_slab.dtype),
            pltpu.VMEM((nrow, rows, nr), jnp.float32),
            pltpu.VMEM((ncol, spo, rows, nr), jnp.float32),
            pltpu.VMEM((nr, 1), jnp.float32),
            pltpu.SemaphoreType.DMA((depth // nvir,)),
            pltpu.SemaphoreType.DMA((nq,)),
            pltpu.SemaphoreType.DMA((3, nrow, nq)),
            pltpu.SemaphoreType.DMA((nrow, nq)),
            pltpu.SemaphoreType.DMA((nrow,)),
            pltpu.SemaphoreType.DMA((ncol, spo)),
        ]
        if nh:
            scratch += [
                pltpu.VMEM((nh, cap, kc), w_slab.dtype),
                pltpu.VMEM((nh, cap, kc), w_slab.dtype),
                pltpu.VMEM((nr, kc), w_slab.dtype),
                pltpu.VMEM((nrow, rows, nr), jnp.float32),
                pltpu.VMEM((nrow, rows, nr), jnp.float32),
                pltpu.VMEM((nr, 1), jnp.float32),
                pltpu.VMEM((nr, cap), w_slab.dtype),
                pltpu.VMEM((cap, nr), w_slab.dtype),
                pltpu.SemaphoreType.DMA((nh,)),
                pltpu.SemaphoreType.DMA((nh,)),
                pltpu.SemaphoreType.DMA((nrow // 2,)),
                pltpu.SemaphoreType.DMA((nrow // 2,)),
            ]
        return pl.pallas_call(
            functools.partial(kernel, nrow, ncol, kc, nh, cap),
            out_shape=jax.ShapeDtypeStruct((spo * rows, nr), jnp.float32),
            in_specs=[pl.BlockSpec(memory_space=pltpu.SMEM), vmem, anywhere, anywhere],
            out_specs=vmem,
            scratch_shapes=scratch,
            compiler_params=pltpu.CompilerParams(
                collective_id=1 if nh else 0, has_side_effects=True, vmem_limit_bytes=58 * 1024 * 1024),
            cost_estimate=pl.CostEstimate(
                flops=2 * nrow * rows * nr * depth, bytes_accessed=2 * nr * depth, transcendentals=0),
        )(*args)

    args = (occ_irrep, vir_irrep.reshape(1, nvir), w_slab, amplitudes)
    if not help_chunks:
        return call(0, *args)
    nocc = -(-nrow * nr // nvir)
    labels = (occ_irrep[:nocc, None] ^ vir_irrep[None, :]).reshape(-1)[:nrow * nr].reshape(nrow, 1, nr)
    counts = jnp.sum(labels == jnp.arange(8, dtype=jnp.int32).reshape(1, 8, 1), axis=2)
    fits = jnp.max(counts) <= cap
    return lax.cond(fits, functools.partial(call, help_chunks), functools.partial(call, 0), *args)


def solution(mesh):
    placed = (P(), P(), P("row", "col"), P("row", "col"))
    shape = dict(mesh.shape)
    return jax.shard_map(
        functools.partial(body, shape["row"], shape["col"]), mesh=mesh,
        in_specs=placed, out_specs=P("col", "row"), check_vma=False)
```

```python
import functools

import jax
import jax.numpy as jnp
from jax import lax
from jax.experimental import pallas as pl
from jax.experimental.pallas import tpu as pltpu
from jax.sharding import PartitionSpec as P
from math import gcd

MESH = pl.DeviceIdType.MESH
NT = (((1,), (1,)), ((), ()))
KC = 2048


def kernel(nrow, ncol, kc, nh, cap, occ_ref, vir_row, w_hbm, a_hbm, out_ref,
           gath, wm, acc, done, red, row_lab, w_sem, own_sem, send_sem, recv_sem, rs_send, rs_recv,
           v_out=None, v_in=None, w_help=None, p_acc=None, p_out=None, p_in=None, help_lab=None,
           spread=None, fold=None, v_send=None, v_recv=None, p_send=None, p_recv=None):
    rho = lax.axis_index("row")
    kap = lax.axis_index("col")
    chips = nrow // 2
    chip = rho // 2
    core = rho % 2
    other = chip * 2 + 1 - core
    rows, depth = a_hbm.shape
    nr = w_hbm.shape[0]
    nvir = vir_row.shape[1]
    nq = depth // kc
    per_q = kc // nvir
    spo = nrow // ncol
    sub = gcd(nr, nvir)
    has_up = chip < chips - 1
    has_down = chip > 0
    if nh:
        first, last = chip == 0, chip == chips - 1
        is_end = first | last
        below, above = chip == 1, chip == chips - 2
        helper = below | above
        up_from = jnp.where(above, nh, 0)
        down_from = jnp.where(below, nh, 0)
        lead = nq - 2 * nh
        helped = jnp.where(below, rho - 2, rho + 2)
        end_chip = jnp.where(below, 0, chips - 1)
        patron = jnp.where(first, rho + 2, rho - 2)
    else:
        up_from = down_from = 0

    def w_copy(j):
        cols = pl.ds(pl.multiple_of(j * nvir, nvir), nvir)
        return pltpu.make_async_copy(w_hbm.at[:, cols], wm.at[:, cols], w_sem.at[j])

    def chunk(q):
        return pl.ds(pl.multiple_of(q * kc, kc), kc)

    def own_copy(q):
        return pltpu.make_async_copy(a_hbm.at[:, chunk(q)], gath.at[rho, :, chunk(q)], own_sem.at[q])

    def remote(way, s, q, own=False):
        target = (rho + 2, rho - 2, other)[way]
        src = a_hbm.at[:, chunk(q)] if own else gath.at[s, :, chunk(q)]
        return pltpu.make_async_remote_copy(
            src_ref=src, dst_ref=gath.at[s, :, chunk(q)],
            send_sem=send_sem.at[way, s, q], recv_sem=recv_sem.at[s, q],
            device_id=(target, kap), device_id_type=MESH)

    def reduce_copy(s):
        return pltpu.make_async_remote_copy(
            src_ref=done.at[s], dst_ref=red.at[kap, s % spo],
            send_sem=rs_send.at[s], recv_sem=rs_recv.at[kap, s % spo],
            device_id=(rho, s // spo), device_id_type=MESH)

    def loop(n, f):
        def step(i, c):
            f(i)
            return c
        lax.fori_loop(0, n, step, 0)

    loop(nq, lambda q: own_copy(q).start())
    loop(nq * per_q, lambda j: w_copy(j).start())

    barrier = pltpu.get_barrier_semaphore()

    @pl.when(has_up)
    def _():
        pl.semaphore_signal(barrier, inc=1, device_id=(rho + 2, kap), device_id_type=MESH)

    @pl.when(has_down)
    def _():
        pl.semaphore_signal(barrier, inc=1, device_id=(rho - 2, kap), device_id_type=MESH)

    pl.semaphore_signal(barrier, inc=1, device_id=(other, kap), device_id_type=MESH)
    for t in range(1, ncol):
        pl.semaphore_signal(barrier, inc=1, device_id=(rho, lax.rem(kap + t, ncol)), device_id_type=MESH)
    pl.semaphore_wait(barrier, ncol + has_up.astype(jnp.int32) + has_down.astype(jnp.int32))

    def send_far(q):
        @pl.when(has_up & (q >= up_from))
        def _():
            remote(0, rho, q, True).start()

        @pl.when(has_down & (q >= down_from))
        def _():
            remote(1, rho, q, True).start()

    def send_own(q):
        remote(2, rho, q, True).start()
        if nh:
            @pl.when((q < lead) | jnp.logical_not(is_end))
            def _():
                send_far(q)
        else:
            send_far(q)

    loop(nq, send_own)
    acc[...] = jnp.zeros_like(acc)

    def lane_labels(owner, b):
        start = owner * nr + b * sub
        at = pl.multiple_of(lax.rem(start, nvir), sub)
        return (vir_row[:, pl.ds(at, sub)] ^ occ_ref[start // nvir]).astype(jnp.float32)

    sub_i = lax.broadcasted_iota(jnp.int32, (sub, sub), 0)
    lane_i = lax.broadcasted_iota(jnp.int32, (sub, sub), 1)

    def write_labels(owner, ref):
        for b in range(nr // sub):
            wide = jnp.broadcast_to(lane_labels(owner, b), (sub, sub))
            ref[b * sub:(b + 1) * sub, :] = jnp.sum(
                jnp.where(sub_i == lane_i, wide, 0.0), axis=1, keepdims=True)

    def col_labels(j):
        return (vir_row[...] ^ occ_ref[kap * (depth // nvir) + j]).astype(jnp.float32)

    write_labels(rho, row_lab)

    def mask(j):
        w_copy(j).wait()
        cols = pl.ds(pl.multiple_of(j * nvir, nvir), nvir)
        labels = col_labels(j)
        for b in range(nr // sub):
            block = wm[b * sub:(b + 1) * sub, cols].astype(jnp.float32)
            kept = jnp.where(row_lab[b * sub:(b + 1) * sub, :] == labels, block, 0.0)
            wm[b * sub:(b + 1) * sub, cols] = kept.astype(wm.dtype)

    if nh:
        def v_copy(g):
            return pltpu.make_async_remote_copy(
                src_ref=v_out.at[g], dst_ref=v_in.at[g],
                send_sem=v_send.at[g], recv_sem=v_recv.at[g],
                device_id=(patron, kap), device_id_type=MESH)

        def p_copy(p):
            at = pl.ds(2 * p, 2)
            return pltpu.make_async_remote_copy(
                src_ref=p_out.at[at], dst_ref=p_in.at[at],
                send_sem=p_send.at[p], recv_sem=p_recv.at[p],
                device_id=(helped, kap), device_id_type=MESH)

        @pl.when(is_end)
        def _():
            for b in range(nr // sub):
                mine = lane_labels(rho, b)
                rank = jnp.zeros((1, sub), jnp.float32)
                for c in range(b + 1):
                    same = row_lab[c * sub:(c + 1) * sub, :] == mine
                    if c == b:
                        same = same & (sub_i < lane_i)
                    rank = rank + jnp.sum(jnp.where(same, 1.0, 0.0), axis=0, keepdims=True)
                slot = lax.broadcasted_iota(jnp.int32, (cap, sub), 0).astype(jnp.float32)
                fold[:, b * sub:(b + 1) * sub] = jnp.where(slot == rank, 1.0, 0.0).astype(fold.dtype)

        @pl.when(helper)
        def _():
            p_acc[...] = jnp.zeros_like(p_acc)
            write_labels(helped, help_lab)
            for b in range(nr // sub):
                mine = help_lab[b * sub:(b + 1) * sub, :]
                rank = jnp.zeros((sub, 1), jnp.float32)
                for c in range(b + 1):
                    same = mine == lane_labels(helped, c)
                    if c == b:
                        same = same & (lane_i < sub_i)
                    rank = rank + jnp.sum(jnp.where(same, 1.0, 0.0), axis=1, keepdims=True)
                slot = lax.broadcasted_iota(jnp.int32, (sub, cap), 1).astype(jnp.float32)
                spread[b * sub:(b + 1) * sub, :] = jnp.where(slot == rank, 1.0, 0.0).astype(spread.dtype)

        def send_folded(g):
            def part(j):
                at = pl.ds(pl.multiple_of(j * nvir, nvir), nvir)
                cols = pl.ds(pl.multiple_of(g * kc + j * nvir, nvir), nvir)
                v = jnp.dot(fold[...], wm[:, cols], preferred_element_type=jnp.float32)
                v_out[g, :, at] = v.astype(v_out.dtype)

            loop(per_q, part)
            v_copy(g).start()
            send_far(lead + 2 * g)
            send_far(lead + 2 * g + 1)

        def help_with(g):
            v_copy(g).wait_recv()

            def part(j):
                at = pl.ds(pl.multiple_of(j * nvir, nvir), nvir)
                labels = col_labels(g * per_q + j)
                for b in range(nr // sub):
                    rows_b = slice(b * sub, (b + 1) * sub)
                    block = jnp.dot(spread[rows_b, :], v_in[g, :, at], preferred_element_type=jnp.float32)
                    kept = jnp.where(help_lab[rows_b, :] == labels, block, 0.0)
                    w_help[rows_b, at] = kept.astype(w_help.dtype)

            loop(per_q, part)

            def one(t):
                p = jnp.where(below, t + 1, t)
                a = gath[pl.ds(2 * p, 2), :, chunk(g)].reshape(2 * rows, kc)
                p_acc[p] += lax.dot_general(w_help[...], a, NT, preferred_element_type=jnp.float32)

                @pl.when(g == nh - 1)
                def _():
                    p_out[pl.ds(2 * p, 2)] = p_acc[p].T.reshape(2, rows, nr)
                    p_copy(p).start()

            loop(chips - 1, one)

    def product(p, q):
        a = gath[pl.ds(2 * p, 2), :, chunk(q)].reshape(2 * rows, kc)
        acc[p] += lax.dot_general(wm[:, chunk(q)], a, NT, preferred_element_type=jnp.float32)

    def finish(p, more=None):
        whole = acc[p].T.reshape(2, rows, nr)
        done[pl.ds(2 * p, 2)] = whole if more is None else whole + more[pl.ds(2 * p, 2)]
        for e in range(2):
            s = 2 * p + e

            @pl.when(s // spo != kap)
            def _():
                reduce_copy(s).start()

    def own_step(q):
        loop(per_q, lambda j: mask(q * per_q + j))
        if nh:
            @pl.when(is_end & (q < nh))
            def _():
                send_folded(q)

        own_copy(q).wait()
        remote(2, other, q).wait_recv()
        product(chip, q)

    loop(nq, own_step)
    finish(chip)

    def source(way, i):
        d = i // nq + 1
        q = i % nq
        p = chip - d if way == 0 else chip + d
        there = p >= 0 if way == 0 else p < chips
        if nh:
            there = there & jnp.logical_not(is_end & (q < nh))
            slow = below if way == 0 else above
            j = jnp.maximum(i - lead + 2, 0)
            g = (2 * j + 1) // 9
            off = j - (9 * g) // 2
            early = i < lead
            later = (i >= lead) & (g >= 1) & (g <= nh) & (off >= 1) & (off <= 2)
            slow_q = jnp.where(early, i, jnp.where(later, lead + 2 * (g - 1) + off - 1, 0))
            p = jnp.where(slow, end_chip, p)
            q = jnp.where(slow, slow_q, q)
            there = (slow & (early | later)) | (jnp.logical_not(slow) & there)
        return p, q, there

    def far_step(i):
        for way in range(2):
            p, q, there = source(way, i)
            onward = has_up & (q >= up_from) if way == 0 else has_down & (q >= down_from)

            @pl.when(there)
            def _():
                s = 2 * p + core
                remote(way, s, q).wait_recv()

                @pl.when(onward)
                def _():
                    remote(way, s, q).start()

                remote(2, s, q).start()

        for way in range(2):
            p, q, there = source(way, i)

            @pl.when(there)
            def _():
                remote(2, 2 * p + 1 - core, q).wait_recv()
                product(p, q)

                @pl.when((q == nq - 1) & jnp.logical_not(is_end) if nh else q == nq - 1)
                def _():
                    finish(p)

        if nh:
            def maybe(g):
                ready = jnp.maximum(lead - 2 + (9 * (g + 1)) // 2, (chips - 3) * nq + g)

                @pl.when(i == ready)
                def _():
                    help_with(g)

            @pl.when(helper)
            def _():
                loop(nh, maybe)

    loop((chips - 1) * nq, far_step)

    if nh:
        @pl.when(is_end)
        def _():
            def settle(t):
                p = jnp.where(first, t + 1, chips - 2 - t)
                at = pl.ds(2 * p, 2)
                pltpu.make_async_remote_copy(
                    src_ref=p_out.at[at], dst_ref=p_in.at[at],
                    send_sem=p_send.at[p], recv_sem=p_recv.at[p],
                    device_id=(patron, kap), device_id_type=MESH).wait_recv()
                finish(p, p_in)

            loop(chips - 1, settle)

    for i in range(spo):
        total = done[kap * spo + i]
        for t in range(1, ncol):
            peer = lax.rem(kap + t, ncol)
            pltpu.make_async_remote_copy(
                src_ref=done.at[i], dst_ref=red.at[peer, i],
                send_sem=rs_send.at[i], recv_sem=rs_recv.at[peer, i],
                device_id=(rho, peer), device_id_type=MESH).wait_recv()
            total = total + red[peer, i]
        out_ref[i * rows:(i + 1) * rows, :] = total

    def drain(i):
        p = i // nq
        q = i % nq
        s = 2 * p + core

        @pl.when(has_up & (p <= chip) & (q >= up_from))
        def _():
            remote(0, s, q).wait_send()

        @pl.when(has_down & (p >= chip) & (q >= down_from))
        def _():
            remote(1, s, q).wait_send()

        @pl.when((p == chip) | jnp.logical_not(is_end & (q < nh)) if nh else p >= 0)
        def _():
            remote(2, s, q).wait_send()

    loop(chips * nq, drain)

    if nh:
        @pl.when(is_end)
        def _():
            loop(nh, lambda g: v_copy(g).wait_send())

        @pl.when(helper)
        def _():
            loop(chips - 1, lambda t: p_copy(jnp.where(below, t + 1, t)).wait_send())

    def drain_reduce(s):
        @pl.when(s // spo != kap)
        def _():
            reduce_copy(s).wait_send()

    loop(nrow, drain_reduce)


def body(nrow, ncol, occ_irrep, vir_irrep, w_slab, amplitudes):
    rows, depth = amplitudes.shape
    nr = w_slab.shape[0]
    nvir = vir_irrep.shape[0]
    kc = KC if depth % KC == 0 else depth
    nq = depth // kc
    spo = nrow // ncol
    cap = -(-nr * 5 // 24 // 16) * 16
    help_chunks = 3 * nq // 8 if nrow // 2 >= 4 else 0
    vmem = pl.BlockSpec(memory_space=pltpu.VMEM)
    anywhere = pl.BlockSpec(memory_space=pl.ANY)

    def call(nh, *args):
        scratch = [
            pltpu.VMEM((nrow, rows, depth), amplitudes.dtype),
            pltpu.VMEM((nr, depth), w_slab.dtype),
            pltpu.VMEM((nrow // 2, nr, 2 * rows), jnp.float32),
            pltpu.VMEM((nrow, rows, nr), jnp.float32),
            pltpu.VMEM((ncol, spo, rows, nr), jnp.float32),
            pltpu.VMEM((nr, 1), jnp.float32),
            pltpu.SemaphoreType.DMA((depth // nvir,)),
            pltpu.SemaphoreType.DMA((nq,)),
            pltpu.SemaphoreType.DMA((3, nrow, nq)),
            pltpu.SemaphoreType.DMA((nrow, nq)),
            pltpu.SemaphoreType.DMA((nrow,)),
            pltpu.SemaphoreType.DMA((ncol, spo)),
        ]
        if nh:
            scratch += [
                pltpu.VMEM((nh, cap, kc), w_slab.dtype),
                pltpu.VMEM((nh, cap, kc), w_slab.dtype),
                pltpu.VMEM((nr, kc), w_slab.dtype),
                pltpu.VMEM((nrow // 2, nr, 2 * rows), jnp.float32),
                pltpu.VMEM((nrow, rows, nr), jnp.float32),
                pltpu.VMEM((nrow, rows, nr), jnp.float32),
                pltpu.VMEM((nr, 1), jnp.float32),
                pltpu.VMEM((nr, cap), w_slab.dtype),
                pltpu.VMEM((cap, nr), w_slab.dtype),
                pltpu.SemaphoreType.DMA((nh,)),
                pltpu.SemaphoreType.DMA((nh,)),
                pltpu.SemaphoreType.DMA((nrow // 2,)),
                pltpu.SemaphoreType.DMA((nrow // 2,)),
            ]
        return pl.pallas_call(
            functools.partial(kernel, nrow, ncol, kc, nh, cap),
            out_shape=jax.ShapeDtypeStruct((spo * rows, nr), jnp.float32),
            in_specs=[pl.BlockSpec(memory_space=pltpu.SMEM), vmem, anywhere, anywhere],
            out_specs=vmem,
            scratch_shapes=scratch,
            compiler_params=pltpu.CompilerParams(
                collective_id=1 if nh else 0, has_side_effects=True, vmem_limit_bytes=58 * 1024 * 1024),
            cost_estimate=pl.CostEstimate(
                flops=2 * nrow * rows * nr * depth, bytes_accessed=2 * nr * depth, transcendentals=0),
        )(*args)

    args = (occ_irrep, vir_irrep.reshape(1, nvir), w_slab, amplitudes)
    if not help_chunks:
        return call(0, *args)
    nocc = -(-nrow * nr // nvir)
    labels = (occ_irrep[:nocc, None] ^ vir_irrep[None, :]).reshape(-1)[:nrow * nr].reshape(nrow, 1, nr)
    counts = jnp.sum(labels == jnp.arange(8, dtype=jnp.int32).reshape(1, 8, 1), axis=2)
    fits = jnp.max(counts) <= cap
    return lax.cond(fits, functools.partial(call, help_chunks), functools.partial(call, 0), *args)


def solution(mesh):
    placed = (P(), P(), P("row", "col"), P("row", "col"))
    shape = dict(mesh.shape)
    return jax.shard_map(
        functools.partial(body, shape["row"], shape["col"]), mesh=mesh,
        in_specs=placed, out_specs=P("col", "row"), check_vma=False)
```

```python
import functools

import jax
import jax.numpy as jnp
from jax import lax
from jax.experimental import pallas as pl
from jax.experimental.pallas import tpu as pltpu
from jax.sharding import PartitionSpec as P
from math import gcd

MESH = pl.DeviceIdType.MESH
NT = (((1,), (1,)), ((), ()))
KC = 2048
AHEAD = 5


def kernel(nrow, ncol, kc, nh, cap, occ_ref, vir_row, w_hbm, a_hbm, out_ref,
           gath, wm, acc, done, red, row_lab, w_sem, own_sem, send_sem, recv_sem, rs_send, rs_recv,
           v_out=None, v_in=None, w_help=None, p_acc=None, p_out=None, p_in=None, help_lab=None,
           spread=None, fold=None, v_send=None, v_recv=None, p_send=None, p_recv=None):
    rho = lax.axis_index("row")
    kap = lax.axis_index("col")
    chips = nrow // 2
    chip = rho // 2
    core = rho % 2
    other = chip * 2 + 1 - core
    rows, depth = a_hbm.shape
    nr = w_hbm.shape[0]
    nvir = vir_row.shape[1]
    nq = depth // kc
    per_q = kc // nvir
    spo = nrow // ncol
    sub = gcd(nr, nvir)
    has_up = chip < chips - 1
    has_down = chip > 0
    if nh:
        first, last = chip == 0, chip == chips - 1
        is_end = first | last
        below, above = chip == 1, chip == chips - 2
        helper = below | above
        up_from = jnp.where(above, nh, 0)
        down_from = jnp.where(below, nh, 0)
        helped = jnp.where(below, rho - 2, rho + 2)
        patron = jnp.where(first, rho + 2, rho - 2)
    else:
        up_from = down_from = 0

    def w_copy(j):
        cols = pl.ds(pl.multiple_of(j * nvir, nvir), nvir)
        return pltpu.make_async_copy(w_hbm.at[:, cols], wm.at[:, cols], w_sem.at[j])

    def chunk(q):
        return pl.ds(pl.multiple_of(q * kc, kc), kc)

    def own_copy(q):
        return pltpu.make_async_copy(a_hbm.at[:, chunk(q)], gath.at[rho, :, chunk(q)], own_sem.at[q])

    def remote(way, s, q, own=False):
        target = (rho + 2, rho - 2, other)[way]
        src = a_hbm.at[:, chunk(q)] if own else gath.at[s, :, chunk(q)]
        return pltpu.make_async_remote_copy(
            src_ref=src, dst_ref=gath.at[s, :, chunk(q)],
            send_sem=send_sem.at[way, s, q], recv_sem=recv_sem.at[s, q],
            device_id=(target, kap), device_id_type=MESH)

    def reduce_copy(s):
        return pltpu.make_async_remote_copy(
            src_ref=done.at[s], dst_ref=red.at[kap, s % spo],
            send_sem=rs_send.at[s], recv_sem=rs_recv.at[kap, s % spo],
            device_id=(rho, s // spo), device_id_type=MESH)

    def loop(n, f):
        def step(i, c):
            f(i)
            return c
        lax.fori_loop(0, n, step, 0)

    loop(nq, lambda q: own_copy(q).start())
    loop(nq * per_q, lambda j: w_copy(j).start())

    barrier = pltpu.get_barrier_semaphore()

    @pl.when(has_up)
    def _():
        pl.semaphore_signal(barrier, inc=1, device_id=(rho + 2, kap), device_id_type=MESH)

    @pl.when(has_down)
    def _():
        pl.semaphore_signal(barrier, inc=1, device_id=(rho - 2, kap), device_id_type=MESH)

    pl.semaphore_signal(barrier, inc=1, device_id=(other, kap), device_id_type=MESH)
    for t in range(1, ncol):
        pl.semaphore_signal(barrier, inc=1, device_id=(rho, lax.rem(kap + t, ncol)), device_id_type=MESH)
    pl.semaphore_wait(barrier, ncol + has_up.astype(jnp.int32) + has_down.astype(jnp.int32))

    ahead = min(AHEAD, nq)

    def counted(n, skip):
        return (n // nq) * (nq - skip) + jnp.maximum(n % nq - skip, 0)

    def sendable(way, n):
        skip = up_from if way == 0 else down_from
        reach = chip + 1 if way == 0 else chips - chip
        seen = counted(n, jnp.where(is_end, nh, 0)) if nh else n
        most = jnp.minimum(nq - skip + counted(n, skip), (nq - skip) * reach)
        most = jnp.minimum(most, ahead + seen)
        return jnp.where(has_up if way == 0 else has_down, most, 0)

    def send_between(way, lo, hi):
        skip = up_from if way == 0 else down_from

        def send(m, c):
            d = lax.div(m, nq - skip)
            q = skip + lax.rem(m, nq - skip)
            p = chip - d if way == 0 else chip + d
            remote(way, 2 * p + core, q).start()
            return c

        lax.fori_loop(lo, hi, send, 0)

    loop(nq, lambda q: own_copy(q).wait())
    for way in range(2):
        send_between(way, 0, sendable(way, 0))
    loop(nq, lambda q: remote(2, rho, q, True).start())
    acc[...] = jnp.zeros_like(acc)

    def lane_labels(owner, b):
        start = owner * nr + b * sub
        at = pl.multiple_of(lax.rem(start, nvir), sub)
        return (vir_row[:, pl.ds(at, sub)] ^ occ_ref[start // nvir]).astype(jnp.float32)

    sub_i = lax.broadcasted_iota(jnp.int32, (sub, sub), 0)
    lane_i = lax.broadcasted_iota(jnp.int32, (sub, sub), 1)

    def write_labels(owner, ref):
        for b in range(nr // sub):
            wide = jnp.broadcast_to(lane_labels(owner, b), (sub, sub))
            ref[b * sub:(b + 1) * sub, :] = jnp.sum(
                jnp.where(sub_i == lane_i, wide, 0.0), axis=1, keepdims=True)

    def col_labels(j):
        return (vir_row[...] ^ occ_ref[kap * (depth // nvir) + j]).astype(jnp.float32)

    write_labels(rho, row_lab)

    def mask(j):
        w_copy(j).wait()
        cols = pl.ds(pl.multiple_of(j * nvir, nvir), nvir)
        labels = col_labels(j)
        for b in range(nr // sub):
            block = wm[b * sub:(b + 1) * sub, cols].astype(jnp.float32)
            kept = jnp.where(row_lab[b * sub:(b + 1) * sub, :] == labels, block, 0.0)
            wm[b * sub:(b + 1) * sub, cols] = kept.astype(wm.dtype)

    if nh:
        def v_copy(g):
            return pltpu.make_async_remote_copy(
                src_ref=v_out.at[g], dst_ref=v_in.at[g],
                send_sem=v_send.at[g], recv_sem=v_recv.at[g],
                device_id=(patron, kap), device_id_type=MESH)

        def p_copy(p):
            at = pl.ds(2 * p, 2)
            return pltpu.make_async_remote_copy(
                src_ref=p_out.at[at], dst_ref=p_in.at[at],
                send_sem=p_send.at[p], recv_sem=p_recv.at[p],
                device_id=(helped, kap), device_id_type=MESH)

        @pl.when(is_end)
        def _():
            for b in range(nr // sub):
                mine = lane_labels(rho, b)
                rank = jnp.zeros((1, sub), jnp.float32)
                for c in range(b + 1):
                    same = row_lab[c * sub:(c + 1) * sub, :] == mine
                    if c == b:
                        same = same & (sub_i < lane_i)
                    rank = rank + jnp.sum(jnp.where(same, 1.0, 0.0), axis=0, keepdims=True)
                slot = lax.broadcasted_iota(jnp.int32, (cap, sub), 0).astype(jnp.float32)
                fold[:, b * sub:(b + 1) * sub] = jnp.where(slot == rank, 1.0, 0.0).astype(fold.dtype)

        @pl.when(helper)
        def _():
            p_acc[...] = jnp.zeros_like(p_acc)
            write_labels(helped, help_lab)
            for b in range(nr // sub):
                mine = help_lab[b * sub:(b + 1) * sub, :]
                rank = jnp.zeros((sub, 1), jnp.float32)
                for c in range(b + 1):
                    same = mine == lane_labels(helped, c)
                    if c == b:
                        same = same & (lane_i < sub_i)
                    rank = rank + jnp.sum(jnp.where(same, 1.0, 0.0), axis=1, keepdims=True)
                slot = lax.broadcasted_iota(jnp.int32, (sub, cap), 1).astype(jnp.float32)
                spread[b * sub:(b + 1) * sub, :] = jnp.where(slot == rank, 1.0, 0.0).astype(spread.dtype)

        def make_folded(g):
            def part(j):
                at = pl.ds(pl.multiple_of(j * nvir, nvir), nvir)
                cols = pl.ds(pl.multiple_of(g * kc + j * nvir, nvir), nvir)
                v = jnp.dot(fold[...], wm[:, cols], preferred_element_type=jnp.float32)
                v_out[g, :, at] = v.astype(v_out.dtype)

            loop(per_q, part)

        def v_ready(n):
            seen = counted(n, nh) - (nq - ahead + 2)
            ready = jnp.clip((seen + 2) // 2, 0, nh)
            return jnp.where(n <= nq, 0, jnp.where(n == (chips - 1) * nq, nh, ready))

        def help_with(g):
            v_copy(g).wait_recv()

            def part(j):
                at = pl.ds(pl.multiple_of(j * nvir, nvir), nvir)
                labels = col_labels(g * per_q + j)
                for b in range(nr // sub):
                    rows_b = slice(b * sub, (b + 1) * sub)
                    block = jnp.dot(spread[rows_b, :], v_in[g, :, at], preferred_element_type=jnp.float32)
                    kept = jnp.where(help_lab[rows_b, :] == labels, block, 0.0)
                    w_help[rows_b, at] = kept.astype(w_help.dtype)

            loop(per_q, part)

            def one(t):
                p = jnp.where(below, t + 1, t)
                a = gath[pl.ds(2 * p, 2), :, chunk(g)].reshape(2 * rows, kc)
                p_acc[p] += lax.dot_general(w_help[...], a, NT, preferred_element_type=jnp.float32)

                @pl.when(g == nh - 1)
                def _():
                    p_out[pl.ds(2 * p, 2)] = p_acc[p].T.reshape(2, rows, nr)
                    p_copy(p).start()

            loop(chips - 1, one)

    def product(p, q):
        a = gath[pl.ds(2 * p, 2), :, chunk(q)].reshape(2 * rows, kc)
        acc[p] += lax.dot_general(wm[:, chunk(q)], a, NT, preferred_element_type=jnp.float32)

    def finish(p, more=None):
        whole = acc[p].T.reshape(2, rows, nr)
        done[pl.ds(2 * p, 2)] = whole if more is None else whole + more[pl.ds(2 * p, 2)]
        for e in range(2):
            s = 2 * p + e

            @pl.when(s // spo != kap)
            def _():
                reduce_copy(s).start()

    def own_step(q):
        loop(per_q, lambda j: mask(q * per_q + j))
        if nh:
            @pl.when(is_end & (q < nh))
            def _():
                make_folded(q)

        remote(2, other, q).wait_recv()
        product(chip, q)

        @pl.when(q == nq - 1)
        def _():
            finish(chip)

    def source(way, i):
        d = i // nq + 1
        q = i % nq
        p = chip - d if way == 0 else chip + d
        there = p >= 0 if way == 0 else p < chips
        if nh:
            there = there & jnp.logical_not(is_end & (q < nh))
        return p, q, there

    def step(i):
        @pl.when(i < nq)
        def _():
            own_step(i)

        for way in range(2):
            p, q, there = source(way, i)

            @pl.when(there)
            def _():
                s = 2 * p + core
                remote(way, s, q).wait_recv()
                remote(2, s, q).start()

        for way in range(2):
            send_between(way, sendable(way, i), sendable(way, i + 1))

        if nh:
            @pl.when(is_end)
            def _():
                def send_v(g, c):
                    v_copy(g).start()
                    return c

                lax.fori_loop(v_ready(i), v_ready(i + 1), send_v, 0)

        for way in range(2):
            p, q, there = source(way, i)

            @pl.when(there)
            def _():
                remote(2, 2 * p + 1 - core, q).wait_recv()
                product(p, q)

                @pl.when((q == nq - 1) & jnp.logical_not(is_end) if nh else q == nq - 1)
                def _():
                    finish(p)

        if nh:
            def maybe(g):
                ready = (chips - 3) * nq + (nq * (g + 1)) // nh - 1

                @pl.when(i == ready)
                def _():
                    help_with(g)

            @pl.when(helper)
            def _():
                loop(nh, maybe)

    loop((chips - 1) * nq, step)

    if nh:
        @pl.when(is_end)
        def _():
            def settle(t):
                p = jnp.where(first, t + 1, chips - 2 - t)
                at = pl.ds(2 * p, 2)
                pltpu.make_async_remote_copy(
                    src_ref=p_out.at[at], dst_ref=p_in.at[at],
                    send_sem=p_send.at[p], recv_sem=p_recv.at[p],
                    device_id=(patron, kap), device_id_type=MESH).wait_recv()
                finish(p, p_in)

            loop(chips - 1, settle)

    for i in range(spo):
        total = done[kap * spo + i]
        for t in range(1, ncol):
            peer = lax.rem(kap + t, ncol)
            pltpu.make_async_remote_copy(
                src_ref=done.at[i], dst_ref=red.at[peer, i],
                send_sem=rs_send.at[i], recv_sem=rs_recv.at[peer, i],
                device_id=(rho, peer), device_id_type=MESH).wait_recv()
            total = total + red[peer, i]
        out_ref[i * rows:(i + 1) * rows, :] = total

    def drain(i):
        p = i // nq
        q = i % nq
        s = 2 * p + core

        @pl.when(has_up & (p <= chip) & (q >= up_from))
        def _():
            remote(0, s, q).wait_send()

        @pl.when(has_down & (p >= chip) & (q >= down_from))
        def _():
            remote(1, s, q).wait_send()

        @pl.when((p == chip) | jnp.logical_not(is_end & (q < nh)) if nh else p >= 0)
        def _():
            remote(2, s, q).wait_send()

    loop(chips * nq, drain)

    if nh:
        @pl.when(is_end)
        def _():
            loop(nh, lambda g: v_copy(g).wait_send())

        @pl.when(helper)
        def _():
            loop(chips - 1, lambda t: p_copy(jnp.where(below, t + 1, t)).wait_send())

    def drain_reduce(s):
        @pl.when(s // spo != kap)
        def _():
            reduce_copy(s).wait_send()

    loop(nrow, drain_reduce)


def body(nrow, ncol, occ_irrep, vir_irrep, w_slab, amplitudes):
    rows, depth = amplitudes.shape
    nr = w_slab.shape[0]
    nvir = vir_irrep.shape[0]
    kc = KC if depth % KC == 0 else depth
    nq = depth // kc
    spo = nrow // ncol
    cap = -(-nr * 5 // 24 // 16) * 16
    help_chunks = 3 * nq // 8 if nrow // 2 >= 4 else 0
    vmem = pl.BlockSpec(memory_space=pltpu.VMEM)
    anywhere = pl.BlockSpec(memory_space=pl.ANY)

    def call(nh, *args):
        scratch = [
            pltpu.VMEM((nrow, rows, depth), amplitudes.dtype),
            pltpu.VMEM((nr, depth), w_slab.dtype),
            pltpu.VMEM((nrow // 2, nr, 2 * rows), jnp.float32),
            pltpu.VMEM((nrow, rows, nr), jnp.float32),
            pltpu.VMEM((ncol, spo, rows, nr), jnp.float32),
            pltpu.VMEM((nr, 1), jnp.float32),
            pltpu.SemaphoreType.DMA((depth // nvir,)),
            pltpu.SemaphoreType.DMA((nq,)),
            pltpu.SemaphoreType.DMA((3, nrow, nq)),
            pltpu.SemaphoreType.DMA((nrow, nq)),
            pltpu.SemaphoreType.DMA((nrow,)),
            pltpu.SemaphoreType.DMA((ncol, spo)),
        ]
        if nh:
            scratch += [
                pltpu.VMEM((nh, cap, kc), w_slab.dtype),
                pltpu.VMEM((nh, cap, kc), w_slab.dtype),
                pltpu.VMEM((nr, kc), w_slab.dtype),
                pltpu.VMEM((nrow // 2, nr, 2 * rows), jnp.float32),
                pltpu.VMEM((nrow, rows, nr), jnp.float32),
                pltpu.VMEM((nrow, rows, nr), jnp.float32),
                pltpu.VMEM((nr, 1), jnp.float32),
                pltpu.VMEM((nr, cap), w_slab.dtype),
                pltpu.VMEM((cap, nr), w_slab.dtype),
                pltpu.SemaphoreType.DMA((nh,)),
                pltpu.SemaphoreType.DMA((nh,)),
                pltpu.SemaphoreType.DMA((nrow // 2,)),
                pltpu.SemaphoreType.DMA((nrow // 2,)),
            ]
        return pl.pallas_call(
            functools.partial(kernel, nrow, ncol, kc, nh, cap),
            out_shape=jax.ShapeDtypeStruct((spo * rows, nr), jnp.float32),
            in_specs=[pl.BlockSpec(memory_space=pltpu.SMEM), vmem, anywhere, anywhere],
            out_specs=vmem,
            scratch_shapes=scratch,
            compiler_params=pltpu.CompilerParams(
                collective_id=1 if nh else 0, has_side_effects=True, vmem_limit_bytes=58 * 1024 * 1024),
            cost_estimate=pl.CostEstimate(
                flops=2 * nrow * rows * nr * depth, bytes_accessed=2 * nr * depth, transcendentals=0),
        )(*args)

    args = (occ_irrep, vir_irrep.reshape(1, nvir), w_slab, amplitudes)
    if not help_chunks:
        return call(0, *args)
    nocc = -(-nrow * nr // nvir)
    labels = (occ_irrep[:nocc, None] ^ vir_irrep[None, :]).reshape(-1)[:nrow * nr].reshape(nrow, 1, nr)
    counts = jnp.sum(labels == jnp.arange(8, dtype=jnp.int32).reshape(1, 8, 1), axis=2)
    fits = jnp.max(counts) <= cap
    return lax.cond(fits, functools.partial(call, help_chunks), functools.partial(call, 0), *args)


def solution(mesh):
    placed = (P(), P(), P("row", "col"), P("row", "col"))
    shape = dict(mesh.shape)
    return jax.shard_map(
        functools.partial(body, shape["row"], shape["col"]), mesh=mesh,
        in_specs=placed, out_specs=P("col", "row"), check_vma=False)
```

```python
import functools

import jax
import jax.numpy as jnp
from jax import lax
from jax.experimental import pallas as pl
from jax.experimental.pallas import tpu as pltpu
from jax.sharding import PartitionSpec as P
from math import gcd

MESH = pl.DeviceIdType.MESH
NT = (((1,), (1,)), ((), ()))
KC = 2048
AHEAD = 5


def kernel(nrow, ncol, kc, nh, cap, occ_ref, vir_row, w_hbm, a_hbm, out_ref,
           gath, wm, acc, near, done, red, row_lab, row_key, w_sem, own_sem, send_sem, recv_sem, rs_send, rs_recv,
           v_out=None, v_in=None, w_help=None, p_acc=None, p_out=None, p_in=None, help_lab=None, help_key=None,
           spread=None, fold=None, v_send=None, v_recv=None, p_send=None, p_recv=None):
    rho = lax.axis_index("row")
    kap = lax.axis_index("col")
    chips = nrow // 2
    chip = rho // 2
    core = rho % 2
    other = chip * 2 + 1 - core
    rows, depth = a_hbm.shape
    nr = w_hbm.shape[0]
    nvir = vir_row.shape[1]
    nq = depth // kc
    per_q = kc // nvir
    spo = nrow // ncol
    sub = gcd(nr, nvir)
    has_up = chip < chips - 1
    has_down = chip > 0
    if nh:
        first, last = chip == 0, chip == chips - 1
        is_end = first | last
        below, above = chip == 1, chip == chips - 2
        helper = below | above
        up_from = jnp.where(above, nh, 0)
        down_from = jnp.where(below, nh, 0)
        helped = jnp.where(below, rho - 2, rho + 2)
        patron = jnp.where(first, rho + 2, rho - 2)
    else:
        up_from = down_from = 0

    def w_copy(j):
        cols = pl.ds(pl.multiple_of(j * nvir, nvir), nvir)
        return pltpu.make_async_copy(w_hbm.at[:, cols], wm.at[:, cols], w_sem.at[j])

    def chunk(q):
        return pl.ds(pl.multiple_of(q * kc, kc), kc)

    def own_copy(q):
        return pltpu.make_async_copy(a_hbm.at[:, chunk(q)], gath.at[rho, :, chunk(q)], own_sem.at[q])

    def remote(way, s, q, own=False):
        target = (rho + 2, rho - 2, other)[way]
        src = a_hbm.at[:, chunk(q)] if own else gath.at[s, :, chunk(q)]
        return pltpu.make_async_remote_copy(
            src_ref=src, dst_ref=gath.at[s, :, chunk(q)],
            send_sem=send_sem.at[way, s, q], recv_sem=recv_sem.at[s, q],
            device_id=(target, kap), device_id_type=MESH)

    def reduce_copy(s):
        return pltpu.make_async_remote_copy(
            src_ref=done.at[s], dst_ref=red.at[kap, s % spo],
            send_sem=rs_send.at[s], recv_sem=rs_recv.at[kap, s % spo],
            device_id=(rho, s // spo), device_id_type=MESH)

    def loop(n, f):
        def step(i, c):
            f(i)
            return c
        lax.fori_loop(0, n, step, 0)

    loop(nq, lambda q: own_copy(q).start())
    loop(nq * per_q, lambda j: w_copy(j).start())

    barrier = pltpu.get_barrier_semaphore()

    @pl.when(has_up)
    def _():
        pl.semaphore_signal(barrier, inc=1, device_id=(rho + 2, kap), device_id_type=MESH)

    @pl.when(has_down)
    def _():
        pl.semaphore_signal(barrier, inc=1, device_id=(rho - 2, kap), device_id_type=MESH)

    pl.semaphore_signal(barrier, inc=1, device_id=(other, kap), device_id_type=MESH)
    for t in range(1, ncol):
        pl.semaphore_signal(barrier, inc=1, device_id=(rho, lax.rem(kap + t, ncol)), device_id_type=MESH)
    pl.semaphore_wait(barrier, ncol + has_up.astype(jnp.int32) + has_down.astype(jnp.int32))

    ahead = min(AHEAD, nq)

    def counted(n, skip):
        return (n // nq) * (nq - skip) + jnp.maximum(n % nq - skip, 0)

    def sendable(way, n):
        skip = up_from if way == 0 else down_from
        reach = chip + 1 if way == 0 else chips - chip
        seen = counted(n, jnp.where(is_end, nh, 0)) if nh else n
        most = jnp.minimum(nq - skip + counted(n, skip), (nq - skip) * reach)
        most = jnp.minimum(most, ahead + seen)
        return jnp.where(has_up if way == 0 else has_down, most, 0)

    def send_between(way, lo, hi):
        skip = up_from if way == 0 else down_from

        def send(m, c):
            d = lax.div(m, nq - skip)
            q = skip + lax.rem(m, nq - skip)
            p = chip - d if way == 0 else chip + d
            remote(way, 2 * p + core, q).start()
            return c

        lax.fori_loop(lo, hi, send, 0)

    loop(nq, lambda q: own_copy(q).wait())
    for way in range(2):
        send_between(way, 0, sendable(way, 0))
    loop(nq, lambda q: remote(2, rho, q, True).start())
    acc[...] = jnp.zeros_like(acc)
    near[...] = jnp.zeros_like(near)

    def lane_labels(owner, b):
        start = owner * nr + b * sub
        at = pl.multiple_of(lax.rem(start, nvir), sub)
        return (vir_row[:, pl.ds(at, sub)] ^ occ_ref[start // nvir]).astype(jnp.float32)

    sub_i = lax.broadcasted_iota(jnp.int32, (sub, sub), 0)
    lane_i = lax.broadcasted_iota(jnp.int32, (sub, sub), 1)

    def write_labels(owner, ref, key):
        for b in range(nr // sub):
            wide = jnp.broadcast_to(lane_labels(owner, b), (sub, sub))
            ref[b * sub:(b + 1) * sub, :] = jnp.sum(
                jnp.where(sub_i == lane_i, wide, 0.0), axis=1, keepdims=True)
        key[...] = jnp.broadcast_to(ref[...], key.shape).astype(key.dtype)

    def col_labels(j):
        return (vir_row[...] ^ occ_ref[kap * (depth // nvir) + j]).astype(jnp.float32).astype(wm.dtype)

    write_labels(rho, row_lab, row_key)

    def keep(key, labels, block):
        key = jnp.concatenate([key] * (nvir // key.shape[1]), axis=1)
        return jnp.where(key == labels, block, jnp.zeros_like(block))

    def mask(j):
        w_copy(j).wait()
        cols = pl.ds(pl.multiple_of(j * nvir, nvir), nvir)
        labels = col_labels(j)
        for b in range(nr // sub):
            block = wm[b * sub:(b + 1) * sub, cols]
            wm[b * sub:(b + 1) * sub, cols] = keep(row_key[b * sub:(b + 1) * sub, :], labels, block)

    if nh:
        def v_copy(g):
            return pltpu.make_async_remote_copy(
                src_ref=v_out.at[g], dst_ref=v_in.at[g],
                send_sem=v_send.at[g], recv_sem=v_recv.at[g],
                device_id=(patron, kap), device_id_type=MESH)

        def p_copy(p):
            at = pl.ds(2 * p, 2)
            return pltpu.make_async_remote_copy(
                src_ref=p_out.at[at], dst_ref=p_in.at[at],
                send_sem=p_send.at[p], recv_sem=p_recv.at[p],
                device_id=(helped, kap), device_id_type=MESH)

        @pl.when(is_end)
        def _():
            for b in range(nr // sub):
                mine = lane_labels(rho, b)
                rank = jnp.zeros((1, sub), jnp.float32)
                for c in range(b + 1):
                    same = row_lab[c * sub:(c + 1) * sub, :] == mine
                    if c == b:
                        same = same & (sub_i < lane_i)
                    rank = rank + jnp.sum(jnp.where(same, 1.0, 0.0), axis=0, keepdims=True)
                slot = lax.broadcasted_iota(jnp.int32, (cap, sub), 0).astype(jnp.float32)
                fold[:, b * sub:(b + 1) * sub] = jnp.where(slot == rank, 1.0, 0.0).astype(fold.dtype)

        @pl.when(helper)
        def _():
            p_acc[...] = jnp.zeros_like(p_acc)
            write_labels(helped, help_lab, help_key)
            for b in range(nr // sub):
                mine = help_lab[b * sub:(b + 1) * sub, :]
                rank = jnp.zeros((sub, 1), jnp.float32)
                for c in range(b + 1):
                    same = mine == lane_labels(helped, c)
                    if c == b:
                        same = same & (lane_i < sub_i)
                    rank = rank + jnp.sum(jnp.where(same, 1.0, 0.0), axis=1, keepdims=True)
                slot = lax.broadcasted_iota(jnp.int32, (sub, cap), 1).astype(jnp.float32)
                spread[b * sub:(b + 1) * sub, :] = jnp.where(slot == rank, 1.0, 0.0).astype(spread.dtype)

        def make_folded(g):
            def part(j):
                at = pl.ds(pl.multiple_of(j * nvir, nvir), nvir)
                cols = pl.ds(pl.multiple_of(g * kc + j * nvir, nvir), nvir)
                v = jnp.dot(fold[...], wm[:, cols], preferred_element_type=jnp.float32)
                v_out[g, :, at] = v.astype(v_out.dtype)

            loop(per_q, part)

        def v_ready(n):
            seen = counted(n, nh) - (nq - ahead + 2)
            ready = jnp.clip((seen + 2) // 2, 0, nh)
            return jnp.where(n <= nq, 0, jnp.where(n == (chips - 1) * nq, nh, ready))

        def help_with(g):
            v_copy(g).wait_recv()

            def part(j):
                at = pl.ds(pl.multiple_of(j * nvir, nvir), nvir)
                labels = col_labels(g * per_q + j)
                for b in range(nr // sub):
                    rows_b = slice(b * sub, (b + 1) * sub)
                    block = jnp.dot(spread[rows_b, :], v_in[g, :, at], preferred_element_type=jnp.float32)
                    w_help[rows_b, at] = keep(help_key[rows_b, :], labels, block.astype(w_help.dtype))

            loop(per_q, part)

            base = jnp.where(below, 2, 0)
            a = gath[pl.ds(base, nrow - 2), :, chunk(g)].reshape((nrow - 2) * rows, kc)
            p_acc[...] += lax.dot_general(w_help[...], a, NT, preferred_element_type=jnp.float32)

            @pl.when(g == nh - 1)
            def _():
                p_out[pl.ds(base, nrow - 2)] = p_acc[...].T.reshape(nrow - 2, rows, nr)
                loop(chips - 1, lambda t: p_copy(jnp.where(below, t + 1, t)).start())

    def product(p, q):
        a = gath[pl.ds(2 * p, 2), :, chunk(q)].reshape(2 * rows, kc)
        acc[p] += lax.dot_general(wm[:, chunk(q)], a, NT, preferred_element_type=jnp.float32)

    def finish(p, more=None):
        whole = acc[p].T.reshape(2, rows, nr)
        done[pl.ds(2 * p, 2)] = whole if more is None else whole + more[pl.ds(2 * p, 2)]
        send_done(p)

    def send_done(p):
        for e in range(2):
            s = 2 * p + e

            @pl.when(s // spo != kap)
            def _():
                reduce_copy(s).start()

    inner = has_up & has_down

    def product_near(q):
        base = 2 * (chip - 1)
        a = gath[pl.ds(base, 6), :, chunk(q)].reshape(6 * rows, kc)
        near[...] += lax.dot_general(wm[:, chunk(q)], a, NT, preferred_element_type=jnp.float32)

        @pl.when(q == nq - 1)
        def _():
            done[pl.ds(base, 6)] = near[...].T.reshape(6, rows, nr)
            loop(3, lambda t: send_done(chip - 1 + t))

    def own_step(q):
        loop(per_q, lambda j: mask(q * per_q + j))
        if nh:
            @pl.when(is_end & (q < nh))
            def _():
                make_folded(q)

        remote(2, other, q).wait_recv()

        @pl.when(jnp.logical_not(inner))
        def _():
            product(chip, q)

            @pl.when(q == nq - 1)
            def _():
                finish(chip)

    def source(way, i):
        d = i // nq + 1
        q = i % nq
        p = chip - d if way == 0 else chip + d
        there = p >= 0 if way == 0 else p < chips
        if nh:
            there = there & jnp.logical_not(is_end & (q < nh))
        return p, q, there

    def step(i):
        @pl.when(i < nq)
        def _():
            own_step(i)

        for way in range(2):
            p, q, there = source(way, i)

            @pl.when(there)
            def _():
                s = 2 * p + core
                remote(way, s, q).wait_recv()
                remote(2, s, q).start()

        for way in range(2):
            send_between(way, sendable(way, i), sendable(way, i + 1))

        if nh:
            @pl.when(is_end)
            def _():
                def send_v(g, c):
                    v_copy(g).start()
                    return c

                lax.fori_loop(v_ready(i), v_ready(i + 1), send_v, 0)

        for way in range(2):
            p, q, there = source(way, i)

            @pl.when(there)
            def _():
                remote(2, 2 * p + 1 - core, q).wait_recv()

                @pl.when(jnp.logical_not(inner & (i < nq)))
                def _():
                    product(p, q)

                    @pl.when((q == nq - 1) & jnp.logical_not(is_end) if nh else q == nq - 1)
                    def _():
                        finish(p)

        @pl.when(inner & (i < nq))
        def _():
            product_near(i)

        if nh:
            def maybe(g):
                ready = (chips - 3) * nq + (nq * (g + 1)) // nh - 1

                @pl.when(i == ready)
                def _():
                    help_with(g)

            @pl.when(helper)
            def _():
                loop(nh, maybe)

    loop((chips - 1) * nq, step)

    if nh:
        @pl.when(is_end)
        def _():
            def settle(t):
                p = jnp.where(first, t + 1, chips - 2 - t)
                at = pl.ds(2 * p, 2)
                pltpu.make_async_remote_copy(
                    src_ref=p_out.at[at], dst_ref=p_in.at[at],
                    send_sem=p_send.at[p], recv_sem=p_recv.at[p],
                    device_id=(patron, kap), device_id_type=MESH).wait_recv()
                finish(p, p_in)

            loop(chips - 1, settle)

    for i in range(spo):
        total = done[kap * spo + i]
        for t in range(1, ncol):
            peer = lax.rem(kap + t, ncol)
            pltpu.make_async_remote_copy(
                src_ref=done.at[i], dst_ref=red.at[peer, i],
                send_sem=rs_send.at[i], recv_sem=rs_recv.at[peer, i],
                device_id=(rho, peer), device_id_type=MESH).wait_recv()
            total = total + red[peer, i]
        out_ref[i * rows:(i + 1) * rows, :] = total

    def drain(i):
        p = i // nq
        q = i % nq
        s = 2 * p + core

        @pl.when(has_up & (p <= chip) & (q >= up_from))
        def _():
            remote(0, s, q).wait_send()

        @pl.when(has_down & (p >= chip) & (q >= down_from))
        def _():
            remote(1, s, q).wait_send()

        @pl.when((p == chip) | jnp.logical_not(is_end & (q < nh)) if nh else p >= 0)
        def _():
            remote(2, s, q).wait_send()

    loop(chips * nq, drain)

    if nh:
        @pl.when(is_end)
        def _():
            loop(nh, lambda g: v_copy(g).wait_send())

        @pl.when(helper)
        def _():
            loop(chips - 1, lambda t: p_copy(jnp.where(below, t + 1, t)).wait_send())

    def drain_reduce(s):
        @pl.when(s // spo != kap)
        def _():
            reduce_copy(s).wait_send()

    loop(nrow, drain_reduce)


def body(nrow, ncol, occ_irrep, vir_irrep, w_slab, amplitudes):
    rows, depth = amplitudes.shape
    nr = w_slab.shape[0]
    nvir = vir_irrep.shape[0]
    kc = KC if depth % KC == 0 else depth
    nq = depth // kc
    spo = nrow // ncol
    cap = -(-nr * 5 // 24 // 16) * 16
    help_chunks = 3 * nq // 8 if nrow // 2 >= 4 else 0
    vmem = pl.BlockSpec(memory_space=pltpu.VMEM)
    anywhere = pl.BlockSpec(memory_space=pl.ANY)

    def call(nh, *args):
        scratch = [
            pltpu.VMEM((nrow, rows, depth), amplitudes.dtype),
            pltpu.VMEM((nr, depth), w_slab.dtype),
            pltpu.VMEM((nrow // 2, nr, 2 * rows), jnp.float32),
            pltpu.VMEM((nr, 6 * rows), jnp.float32),
            pltpu.VMEM((nrow, rows, nr), jnp.float32),
            pltpu.VMEM((ncol, spo, rows, nr), jnp.float32),
            pltpu.VMEM((nr, 1), jnp.float32),
            pltpu.VMEM((nr, 128), w_slab.dtype),
            pltpu.SemaphoreType.DMA((depth // nvir,)),
            pltpu.SemaphoreType.DMA((nq,)),
            pltpu.SemaphoreType.DMA((3, nrow, nq)),
            pltpu.SemaphoreType.DMA((nrow, nq)),
            pltpu.SemaphoreType.DMA((nrow,)),
            pltpu.SemaphoreType.DMA((ncol, spo)),
        ]
        if nh:
            scratch += [
                pltpu.VMEM((nh, cap, kc), w_slab.dtype),
                pltpu.VMEM((nh, cap, kc), w_slab.dtype),
                pltpu.VMEM((nr, kc), w_slab.dtype),
                pltpu.VMEM((nr, (nrow - 2) * rows), jnp.float32),
                pltpu.VMEM((nrow, rows, nr), jnp.float32),
                pltpu.VMEM((nrow, rows, nr), jnp.float32),
                pltpu.VMEM((nr, 1), jnp.float32),
                pltpu.VMEM((nr, 128), w_slab.dtype),
                pltpu.VMEM((nr, cap), w_slab.dtype),
                pltpu.VMEM((cap, nr), w_slab.dtype),
                pltpu.SemaphoreType.DMA((nh,)),
                pltpu.SemaphoreType.DMA((nh,)),
                pltpu.SemaphoreType.DMA((nrow // 2,)),
                pltpu.SemaphoreType.DMA((nrow // 2,)),
            ]
        return pl.pallas_call(
            functools.partial(kernel, nrow, ncol, kc, nh, cap),
            out_shape=jax.ShapeDtypeStruct((spo * rows, nr), jnp.float32),
            in_specs=[pl.BlockSpec(memory_space=pltpu.SMEM), vmem, anywhere, anywhere],
            out_specs=vmem,
            scratch_shapes=scratch,
            compiler_params=pltpu.CompilerParams(
                collective_id=1 if nh else 0, has_side_effects=True, vmem_limit_bytes=58 * 1024 * 1024),
            cost_estimate=pl.CostEstimate(
                flops=2 * nrow * rows * nr * depth, bytes_accessed=2 * nr * depth, transcendentals=0),
        )(*args)

    args = (occ_irrep, vir_irrep.reshape(1, nvir), w_slab, amplitudes)
    if not help_chunks:
        return call(0, *args)
    nocc = -(-nrow * nr // nvir)
    labels = (occ_irrep[:nocc, None] ^ vir_irrep[None, :]).reshape(-1)[:nrow * nr].reshape(nrow, 1, nr)
    counts = jnp.sum(labels == jnp.arange(8, dtype=jnp.int32).reshape(1, 8, 1), axis=2)
    fits = jnp.max(counts) <= cap
    return lax.cond(fits, functools.partial(call, help_chunks), functools.partial(call, 0), *args)


def solution(mesh):
    placed = (P(), P(), P("row", "col"), P("row", "col"))
    shape = dict(mesh.shape)
    return jax.shard_map(
        functools.partial(body, shape["row"], shape["col"]), mesh=mesh,
        in_specs=placed, out_specs=P("col", "row"), check_vma=False)
```

```python
import functools

import jax
import jax.numpy as jnp
from jax import lax
from jax.experimental import pallas as pl
from jax.experimental.pallas import tpu as pltpu
from jax.sharding import PartitionSpec as P
from math import gcd

MESH = pl.DeviceIdType.MESH
NT = (((1,), (1,)), ((), ()))
KC = 2048
AHEAD = 5


def kernel(nrow, ncol, kc, nh, cap, occ_ref, vir_row, w_hbm, a_hbm, out_ref,
           gath, wm, acc, near, done, red, row_lab, row_key, w_sem, own_sem, send_sem, recv_sem, rs_send, rs_recv,
           v_out=None, v_in=None, w_help=None, p_acc=None, p_out=None, p_in=None, help_lab=None, help_key=None,
           spread=None, fold=None, v_send=None, v_recv=None, p_send=None, p_recv=None):
    rho = lax.axis_index("row")
    kap = lax.axis_index("col")
    chips = nrow // 2
    chip = rho // 2
    core = rho % 2
    other = chip * 2 + 1 - core
    rows, depth = a_hbm.shape
    nr = w_hbm.shape[0]
    nvir = vir_row.shape[1]
    nq = depth // kc
    per_q = kc // nvir
    spo = nrow // ncol
    sub = gcd(nr, nvir)
    has_up = chip < chips - 1
    has_down = chip > 0
    if nh:
        first, last = chip == 0, chip == chips - 1
        is_end = first | last
        below, above = chip == 1, chip == chips - 2
        helper = below | above
        up_from = jnp.where(above, nh, 0)
        down_from = jnp.where(below, nh, 0)
        helped = jnp.where(below, rho - 2, rho + 2)
        patron = jnp.where(first, rho + 2, rho - 2)
    else:
        up_from = down_from = 0

    def w_copy(j):
        cols = pl.ds(pl.multiple_of(j * nvir, nvir), nvir)
        return pltpu.make_async_copy(w_hbm.at[:, cols], wm.at[:, cols], w_sem.at[j])

    def chunk(q):
        return pl.ds(pl.multiple_of(q * kc, kc), kc)

    def own_copy(q):
        return pltpu.make_async_copy(a_hbm.at[:, chunk(q)], gath.at[rho, :, chunk(q)], own_sem.at[q])

    def remote(way, s, q, own=False):
        target = (rho + 2, rho - 2, other)[way]
        src = a_hbm.at[:, chunk(q)] if own else gath.at[s, :, chunk(q)]
        return pltpu.make_async_remote_copy(
            src_ref=src, dst_ref=gath.at[s, :, chunk(q)],
            send_sem=send_sem.at[way, s, q], recv_sem=recv_sem.at[s, q],
            device_id=(target, kap), device_id_type=MESH)

    def reduce_copy(s):
        return pltpu.make_async_remote_copy(
            src_ref=done.at[s], dst_ref=red.at[kap, s % spo],
            send_sem=rs_send.at[s], recv_sem=rs_recv.at[kap, s % spo],
            device_id=(rho, s // spo), device_id_type=MESH)

    def loop(n, f):
        def step(i, c):
            f(i)
            return c
        lax.fori_loop(0, n, step, 0)

    loop(nq, lambda q: own_copy(q).start())
    loop(nq * per_q, lambda j: w_copy(j).start())

    barrier = pltpu.get_barrier_semaphore()

    @pl.when(has_up)
    def _():
        pl.semaphore_signal(barrier, inc=1, device_id=(rho + 2, kap), device_id_type=MESH)

    @pl.when(has_down)
    def _():
        pl.semaphore_signal(barrier, inc=1, device_id=(rho - 2, kap), device_id_type=MESH)

    pl.semaphore_signal(barrier, inc=1, device_id=(other, kap), device_id_type=MESH)
    for t in range(1, ncol):
        pl.semaphore_signal(barrier, inc=1, device_id=(rho, lax.rem(kap + t, ncol)), device_id_type=MESH)
    pl.semaphore_wait(barrier, ncol + has_up.astype(jnp.int32) + has_down.astype(jnp.int32))

    ahead = min(AHEAD, nq)

    def counted(n, skip):
        return (n // nq) * (nq - skip) + jnp.maximum(n % nq - skip, 0)

    def slow(x):
        tail = nq // 4
        lead = nq - nh - tail
        between = jnp.clip((2 * (x - lead)) // 7, 0, nh)
        return jnp.minimum(x, lead) + between + jnp.clip(x - lead - (7 * nh) // 2, 0, tail)

    def sendable(way, n):
        skip = up_from if way == 0 else down_from
        reach = chip + 1 if way == 0 else chips - chip
        passed = counted(n, skip)
        if nh:
            passed = jnp.where(below if way == 0 else above, slow(n), passed)
        most = jnp.minimum(nq - skip + passed, (nq - skip) * reach)
        limit = ahead + n
        if nh:
            limit = jnp.where(is_end, slow(ahead + 2 + counted(n, nh)), limit)
        most = jnp.minimum(most, limit)
        return jnp.where(has_up if way == 0 else has_down, most, 0)

    def send_between(way, lo, hi):
        skip = up_from if way == 0 else down_from

        def send(m, c):
            d = lax.div(m, nq - skip)
            q = skip + lax.rem(m, nq - skip)
            p = chip - d if way == 0 else chip + d
            remote(way, 2 * p + core, q).start()
            return c

        lax.fori_loop(lo, hi, send, 0)

    loop(nq, lambda q: own_copy(q).wait())
    for way in range(2):
        send_between(way, 0, sendable(way, 0))
    loop(nq, lambda q: remote(2, rho, q, True).start())
    acc[...] = jnp.zeros_like(acc)
    near[...] = jnp.zeros_like(near)

    def lane_labels(owner, b):
        start = owner * nr + b * sub
        at = pl.multiple_of(lax.rem(start, nvir), sub)
        return (vir_row[:, pl.ds(at, sub)] ^ occ_ref[start // nvir]).astype(jnp.float32)

    sub_i = lax.broadcasted_iota(jnp.int32, (sub, sub), 0)
    lane_i = lax.broadcasted_iota(jnp.int32, (sub, sub), 1)

    def write_labels(owner, ref, key):
        for b in range(nr // sub):
            wide = jnp.broadcast_to(lane_labels(owner, b), (sub, sub))
            ref[b * sub:(b + 1) * sub, :] = jnp.sum(
                jnp.where(sub_i == lane_i, wide, 0.0), axis=1, keepdims=True)
        key[...] = jnp.broadcast_to(ref[...], key.shape).astype(key.dtype)

    def col_labels(j):
        return (vir_row[...] ^ occ_ref[kap * (depth // nvir) + j]).astype(jnp.float32).astype(wm.dtype)

    write_labels(rho, row_lab, row_key)

    def keep(key, labels, block):
        key = jnp.concatenate([key] * (nvir // key.shape[1]), axis=1)
        return jnp.where(key == labels, block, jnp.zeros_like(block))

    def mask(j):
        w_copy(j).wait()
        cols = pl.ds(pl.multiple_of(j * nvir, nvir), nvir)
        labels = col_labels(j)
        for b in range(nr // sub):
            block = wm[b * sub:(b + 1) * sub, cols]
            wm[b * sub:(b + 1) * sub, cols] = keep(row_key[b * sub:(b + 1) * sub, :], labels, block)

    if nh:
        def v_copy(g):
            return pltpu.make_async_remote_copy(
                src_ref=v_out.at[g], dst_ref=v_in.at[g],
                send_sem=v_send.at[g], recv_sem=v_recv.at[g],
                device_id=(patron, kap), device_id_type=MESH)

        def p_copy(p):
            at = pl.ds(2 * p, 2)
            return pltpu.make_async_remote_copy(
                src_ref=p_out.at[at], dst_ref=p_in.at[at],
                send_sem=p_send.at[p], recv_sem=p_recv.at[p],
                device_id=(helped, kap), device_id_type=MESH)

        @pl.when(is_end)
        def _():
            for b in range(nr // sub):
                mine = lane_labels(rho, b)
                rank = jnp.zeros((1, sub), jnp.float32)
                for c in range(b + 1):
                    same = row_lab[c * sub:(c + 1) * sub, :] == mine
                    if c == b:
                        same = same & (sub_i < lane_i)
                    rank = rank + jnp.sum(jnp.where(same, 1.0, 0.0), axis=0, keepdims=True)
                slot = lax.broadcasted_iota(jnp.int32, (cap, sub), 0).astype(jnp.float32)
                fold[:, b * sub:(b + 1) * sub] = jnp.where(slot == rank, 1.0, 0.0).astype(fold.dtype)

        @pl.when(helper)
        def _():
            p_acc[...] = jnp.zeros_like(p_acc)
            write_labels(helped, help_lab, help_key)
            for b in range(nr // sub):
                mine = help_lab[b * sub:(b + 1) * sub, :]
                rank = jnp.zeros((sub, 1), jnp.float32)
                for c in range(b + 1):
                    same = mine == lane_labels(helped, c)
                    if c == b:
                        same = same & (lane_i < sub_i)
                    rank = rank + jnp.sum(jnp.where(same, 1.0, 0.0), axis=1, keepdims=True)
                slot = lax.broadcasted_iota(jnp.int32, (sub, cap), 1).astype(jnp.float32)
                spread[b * sub:(b + 1) * sub, :] = jnp.where(slot == rank, 1.0, 0.0).astype(spread.dtype)

        def make_folded(g):
            def part(j):
                at = pl.ds(pl.multiple_of(j * nvir, nvir), nvir)
                cols = pl.ds(pl.multiple_of(g * kc + j * nvir, nvir), nvir)
                v = jnp.dot(fold[...], wm[:, cols], preferred_element_type=jnp.float32)
                v_out[g, :, at] = v.astype(v_out.dtype)

            loop(per_q, part)

        def v_ready(n):
            x = ahead + 2 + counted(n, nh) - (nq - nh - nq // 4)
            return jnp.clip((2 * x + 2) // 7, 0, nh)

        def help_with(g):
            v_copy(g).wait_recv()

            def part(j):
                at = pl.ds(pl.multiple_of(j * nvir, nvir), nvir)
                labels = col_labels(g * per_q + j)
                for b in range(nr // sub):
                    rows_b = slice(b * sub, (b + 1) * sub)
                    block = jnp.dot(spread[rows_b, :], v_in[g, :, at], preferred_element_type=jnp.float32)
                    w_help[rows_b, at] = keep(help_key[rows_b, :], labels, block.astype(w_help.dtype))

            loop(per_q, part)

            base = jnp.where(below, 2, 0)
            a = gath[pl.ds(base, nrow - 2), :, chunk(g)].reshape((nrow - 2) * rows, kc)
            p_acc[...] += lax.dot_general(w_help[...], a, NT, preferred_element_type=jnp.float32)

            @pl.when(g == nh - 1)
            def _():
                p_out[pl.ds(base, nrow - 2)] = p_acc[...].T.reshape(nrow - 2, rows, nr)
                loop(chips - 1, lambda t: p_copy(jnp.where(below, t + 1, t)).start())

    def product(p, q):
        a = gath[pl.ds(2 * p, 2), :, chunk(q)].reshape(2 * rows, kc)
        acc[p] += lax.dot_general(wm[:, chunk(q)], a, NT, preferred_element_type=jnp.float32)

    def finish(p, more=None):
        whole = acc[p].T.reshape(2, rows, nr)
        done[pl.ds(2 * p, 2)] = whole if more is None else whole + more[pl.ds(2 * p, 2)]
        send_done(p)

    def send_done(p):
        for e in range(2):
            s = 2 * p + e

            @pl.when(s // spo != kap)
            def _():
                reduce_copy(s).start()

    inner = has_up & has_down

    def product_near(q):
        wide = nrow if nh else 6
        base = 0 if nh else 2 * (chip - 1)
        a = gath[pl.ds(base, wide), :, chunk(q)].reshape(wide * rows, kc)
        near[...] += lax.dot_general(wm[:, chunk(q)], a, NT, preferred_element_type=jnp.float32)

        @pl.when(q == nq - 1)
        def _():
            done[pl.ds(base, wide)] = near[...].T.reshape(wide, rows, nr)
            loop(wide // 2, lambda t: send_done(base // 2 + t))

    def own_step(q):
        loop(per_q, lambda j: mask(q * per_q + j))
        if nh:
            @pl.when(is_end & (q < nh))
            def _():
                make_folded(q)

        remote(2, other, q).wait_recv()

        @pl.when(jnp.logical_not(inner))
        def _():
            product(chip, q)

            @pl.when(q == nq - 1)
            def _():
                finish(chip)

    def source(way, i):
        d = i // nq + 1
        q = i % nq
        p = chip - d if way == 0 else chip + d
        there = p >= 0 if way == 0 else p < chips
        if nh:
            there = there & jnp.logical_not(is_end & (q < nh))
            there = there & jnp.logical_not(below if way == 0 else above)
        return p, q, there

    def settle(t):
        p = jnp.where(first, t + 1, chips - 2 - t)
        at = pl.ds(2 * p, 2)
        pltpu.make_async_remote_copy(
            src_ref=p_out.at[at], dst_ref=p_in.at[at],
            send_sem=p_send.at[p], recv_sem=p_recv.at[p],
            device_id=(patron, kap), device_id_type=MESH).wait_recv()
        finish(p, p_in)

    def slow_loop(i, f):
        def one(q, c):
            f(jnp.where(below, core, nrow - 2 + core), q)
            return c

        lax.fori_loop(jnp.where(helper, slow(i), 0), jnp.where(helper, slow(i + 1), 0), one, 0)

    def step(i):
        @pl.when(i < nq)
        def _():
            own_step(i)

        if nh:
            @pl.when(is_end & (i == (chips - 1) * nq - 1))
            def _():
                loop(chips - 2, settle)

        for way in range(2):
            p, q, there = source(way, i)

            @pl.when(there)
            def _():
                s = 2 * p + core
                remote(way, s, q).wait_recv()
                remote(2, s, q).start()

        if nh:
            def take(s, q):
                remote(0, s, q).wait_recv()
                remote(2, s, q).start()

            slow_loop(i, take)

        for way in range(2):
            send_between(way, sendable(way, i), sendable(way, i + 1))

        if nh:
            @pl.when(is_end)
            def _():
                def send_v(g, c):
                    v_copy(g).start()
                    return c

                lax.fori_loop(v_ready(i), v_ready(i + 1), send_v, 0)

        for way in range(2):
            p, q, there = source(way, i)

            @pl.when(there)
            def _():
                remote(2, 2 * p + 1 - core, q).wait_recv()

                @pl.when(is_end if nh else jnp.logical_not(inner & (i < nq)))
                def _():
                    product(p, q)

                    @pl.when((q == nq - 1) & jnp.logical_not(is_end) if nh else q == nq - 1)
                    def _():
                        finish(p)

        if nh:
            slow_loop(i, lambda s, q: remote(2, s + 1 - 2 * core, q).wait_recv())

            @pl.when(inner & (i >= nq) & (i < 2 * nq))
            def _():
                product_near(i - nq)
        else:
            @pl.when(inner & (i < nq))
            def _():
                product_near(i)

        if nh:
            def maybe(g):
                ready = jnp.maximum(nq + g + 1, (2 * (nq - nh - nq // 4) + 7 * g + 6) // 2 - 1)

                @pl.when(i == ready)
                def _():
                    help_with(g)

            @pl.when(helper)
            def _():
                loop(nh, maybe)

    loop((chips - 1) * nq, step)

    if nh:
        @pl.when(is_end)
        def _():
            settle(chips - 2)

    for i in range(spo):
        total = done[kap * spo + i]
        for t in range(1, ncol):
            peer = lax.rem(kap + t, ncol)
            pltpu.make_async_remote_copy(
                src_ref=done.at[i], dst_ref=red.at[peer, i],
                send_sem=rs_send.at[i], recv_sem=rs_recv.at[peer, i],
                device_id=(rho, peer), device_id_type=MESH).wait_recv()
            total = total + red[peer, i]
        out_ref[i * rows:(i + 1) * rows, :] = total

    def drain(i):
        p = i // nq
        q = i % nq
        s = 2 * p + core

        @pl.when(has_up & (p <= chip) & (q >= up_from))
        def _():
            remote(0, s, q).wait_send()

        @pl.when(has_down & (p >= chip) & (q >= down_from))
        def _():
            remote(1, s, q).wait_send()

        @pl.when((p == chip) | jnp.logical_not(is_end & (q < nh)) if nh else p >= 0)
        def _():
            remote(2, s, q).wait_send()

    loop(chips * nq, drain)

    if nh:
        @pl.when(is_end)
        def _():
            loop(nh, lambda g: v_copy(g).wait_send())

        @pl.when(helper)
        def _():
            loop(chips - 1, lambda t: p_copy(jnp.where(below, t + 1, t)).wait_send())

    def drain_reduce(s):
        @pl.when(s // spo != kap)
        def _():
            reduce_copy(s).wait_send()

    loop(nrow, drain_reduce)


def body(nrow, ncol, occ_irrep, vir_irrep, w_slab, amplitudes):
    rows, depth = amplitudes.shape
    nr = w_slab.shape[0]
    nvir = vir_irrep.shape[0]
    kc = KC if depth % KC == 0 else depth
    nq = depth // kc
    spo = nrow // ncol
    cap = -(-nr * 5 // 24 // 16) * 16
    help_chunks = 3 * nq // 8 if nrow // 2 == 4 else 0
    vmem = pl.BlockSpec(memory_space=pltpu.VMEM)
    anywhere = pl.BlockSpec(memory_space=pl.ANY)

    def call(nh, *args):
        scratch = [
            pltpu.VMEM((nrow, rows, depth), amplitudes.dtype),
            pltpu.VMEM((nr, depth), w_slab.dtype),
            pltpu.VMEM((nrow // 2, nr, 2 * rows), jnp.float32),
            pltpu.VMEM((nr, (nrow if nh else 6) * rows), jnp.float32),
            pltpu.VMEM((nrow, rows, nr), jnp.float32),
            pltpu.VMEM((ncol, spo, rows, nr), jnp.float32),
            pltpu.VMEM((nr, 1), jnp.float32),
            pltpu.VMEM((nr, 128), w_slab.dtype),
            pltpu.SemaphoreType.DMA((depth // nvir,)),
            pltpu.SemaphoreType.DMA((nq,)),
            pltpu.SemaphoreType.DMA((3, nrow, nq)),
            pltpu.SemaphoreType.DMA((nrow, nq)),
            pltpu.SemaphoreType.DMA((nrow,)),
            pltpu.SemaphoreType.DMA((ncol, spo)),
        ]
        if nh:
            scratch += [
                pltpu.VMEM((nh, cap, kc), w_slab.dtype),
                pltpu.VMEM((nh, cap, kc), w_slab.dtype),
                pltpu.VMEM((nr, kc), w_slab.dtype),
                pltpu.VMEM((nr, (nrow - 2) * rows), jnp.float32),
                pltpu.VMEM((nrow, rows, nr), jnp.float32),
                pltpu.VMEM((nrow, rows, nr), jnp.float32),
                pltpu.VMEM((nr, 1), jnp.float32),
                pltpu.VMEM((nr, 128), w_slab.dtype),
                pltpu.VMEM((nr, cap), w_slab.dtype),
                pltpu.VMEM((cap, nr), w_slab.dtype),
                pltpu.SemaphoreType.DMA((nh,)),
                pltpu.SemaphoreType.DMA((nh,)),
                pltpu.SemaphoreType.DMA((nrow // 2,)),
                pltpu.SemaphoreType.DMA((nrow // 2,)),
            ]
        return pl.pallas_call(
            functools.partial(kernel, nrow, ncol, kc, nh, cap),
            out_shape=jax.ShapeDtypeStruct((spo * rows, nr), jnp.float32),
            in_specs=[pl.BlockSpec(memory_space=pltpu.SMEM), vmem, anywhere, anywhere],
            out_specs=vmem,
            scratch_shapes=scratch,
            compiler_params=pltpu.CompilerParams(
                collective_id=1 if nh else 0, has_side_effects=True, vmem_limit_bytes=58 * 1024 * 1024),
            cost_estimate=pl.CostEstimate(
                flops=2 * nrow * rows * nr * depth, bytes_accessed=2 * nr * depth, transcendentals=0),
        )(*args)

    args = (occ_irrep, vir_irrep.reshape(1, nvir), w_slab, amplitudes)
    if not help_chunks:
        return call(0, *args)
    nocc = -(-nrow * nr // nvir)
    labels = (occ_irrep[:nocc, None] ^ vir_irrep[None, :]).reshape(-1)[:nrow * nr].reshape(nrow, 1, nr)
    counts = jnp.sum(labels == jnp.arange(8, dtype=jnp.int32).reshape(1, 8, 1), axis=2)
    fits = jnp.max(counts) <= cap
    return lax.cond(fits, functools.partial(call, help_chunks), functools.partial(call, 0), *args)


def solution(mesh):
    placed = (P(), P(), P("row", "col"), P("row", "col"))
    shape = dict(mesh.shape)
    return jax.shard_map(
        functools.partial(body, shape["row"], shape["col"]), mesh=mesh,
        in_specs=placed, out_specs=P("col", "row"), check_vma=False)
```

```python
import functools

import jax
import jax.numpy as jnp
from jax import lax
from jax.experimental import pallas as pl
from jax.experimental.pallas import tpu as pltpu
from jax.sharding import PartitionSpec as P
from math import gcd

MESH = pl.DeviceIdType.MESH
NT = (((1,), (1,)), ((), ()))
KC = 2048
AHEAD = 5


def kernel(nrow, ncol, kc, nh, cap, occ_ref, vir_row, w_hbm, a_hbm, out_ref,
           gath, wm, acc, near, done, red, row_lab, row_key, w_sem, own_sem, send_sem, recv_sem, rs_send, rs_recv,
           v_out=None, v_in=None, w_help=None, p_acc=None, p_out=None, p_in=None, help_lab=None, help_key=None,
           spread=None, fold=None, v_send=None, v_recv=None, p_send=None, p_recv=None):
    rho = lax.axis_index("row")
    kap = lax.axis_index("col")
    chips = nrow // 2
    chip = rho // 2
    core = rho % 2
    other = chip * 2 + 1 - core
    rows, depth = a_hbm.shape
    nr = w_hbm.shape[0]
    nvir = vir_row.shape[1]
    nq = depth // kc
    per_q = kc // nvir
    spo = nrow // ncol
    sub = gcd(nr, nvir)
    has_up = chip < chips - 1
    has_down = chip > 0
    if nh:
        first, last = chip == 0, chip == chips - 1
        is_end = first | last
        below, above = chip == 1, chip == chips - 2
        helper = below | above
        up_from = jnp.where(above, nh, 0)
        down_from = jnp.where(below, nh, 0)
        helped = jnp.where(below, rho - 2, rho + 2)
        patron = jnp.where(first, rho + 2, rho - 2)
    else:
        up_from = down_from = 0

    def w_copy(j):
        cols = pl.ds(pl.multiple_of(j * nvir, nvir), nvir)
        return pltpu.make_async_copy(w_hbm.at[:, cols], wm.at[:, cols], w_sem.at[j])

    def chunk(q):
        return pl.ds(pl.multiple_of(q * kc, kc), kc)

    def own_copy(q):
        return pltpu.make_async_copy(a_hbm.at[:, chunk(q)], gath.at[rho, :, chunk(q)], own_sem.at[q])

    def remote(way, s, q, own=False):
        target = (rho + 2, rho - 2, other)[way]
        src = a_hbm.at[:, chunk(q)] if own else gath.at[s, :, chunk(q)]
        return pltpu.make_async_remote_copy(
            src_ref=src, dst_ref=gath.at[s, :, chunk(q)],
            send_sem=send_sem.at[way, s, q], recv_sem=recv_sem.at[s, q],
            device_id=(target, kap), device_id_type=MESH)

    def reduce_copy(s):
        return pltpu.make_async_remote_copy(
            src_ref=done.at[s], dst_ref=red.at[kap, s % spo],
            send_sem=rs_send.at[s], recv_sem=rs_recv.at[kap, s % spo],
            device_id=(rho, s // spo), device_id_type=MESH)

    def loop(n, f):
        def step(i, c):
            f(i)
            return c
        lax.fori_loop(0, n, step, 0)

    loop(nq, lambda q: own_copy(q).start())
    loop(nq * per_q, lambda j: w_copy(j).start())

    barrier = pltpu.get_barrier_semaphore()

    @pl.when(has_up)
    def _():
        pl.semaphore_signal(barrier, inc=1, device_id=(rho + 2, kap), device_id_type=MESH)

    @pl.when(has_down)
    def _():
        pl.semaphore_signal(barrier, inc=1, device_id=(rho - 2, kap), device_id_type=MESH)

    pl.semaphore_signal(barrier, inc=1, device_id=(other, kap), device_id_type=MESH)
    for t in range(1, ncol):
        pl.semaphore_signal(barrier, inc=1, device_id=(rho, lax.rem(kap + t, ncol)), device_id_type=MESH)
    pl.semaphore_wait(barrier, ncol + has_up.astype(jnp.int32) + has_down.astype(jnp.int32))

    ahead = min(AHEAD, nq)

    def counted(n, skip):
        return (n // nq) * (nq - skip) + jnp.maximum(n % nq - skip, 0)

    def sendable(way, n):
        skip = up_from if way == 0 else down_from
        reach = chip + 1 if way == 0 else chips - chip
        seen = counted(n, jnp.where(is_end, nh, 0)) if nh else n
        most = jnp.minimum(nq - skip + counted(n, skip), (nq - skip) * reach)
        most = jnp.minimum(most, ahead + seen)
        return jnp.where(has_up if way == 0 else has_down, most, 0)

    def send_between(way, lo, hi):
        skip = up_from if way == 0 else down_from

        def send(m, c):
            d = lax.div(m, nq - skip)
            q = skip + lax.rem(m, nq - skip)
            p = chip - d if way == 0 else chip + d
            remote(way, 2 * p + core, q).start()
            return c

        lax.fori_loop(lo, hi, send, 0)

    loop(nq, lambda q: own_copy(q).wait())
    for way in range(2):
        send_between(way, 0, sendable(way, 0))
    loop(nq, lambda q: remote(2, rho, q, True).start())
    acc[...] = jnp.zeros_like(acc)
    near[...] = jnp.zeros_like(near)

    def lane_labels(owner, b):
        start = owner * nr + b * sub
        at = pl.multiple_of(lax.rem(start, nvir), sub)
        return (vir_row[:, pl.ds(at, sub)] ^ occ_ref[start // nvir]).astype(jnp.float32)

    sub_i = lax.broadcasted_iota(jnp.int32, (sub, sub), 0)
    lane_i = lax.broadcasted_iota(jnp.int32, (sub, sub), 1)

    def write_labels(owner, ref, key):
        for b in range(nr // sub):
            wide = jnp.broadcast_to(lane_labels(owner, b), (sub, sub))
            ref[b * sub:(b + 1) * sub, :] = jnp.sum(
                jnp.where(sub_i == lane_i, wide, 0.0), axis=1, keepdims=True)
        key[...] = jnp.broadcast_to(ref[...], key.shape).astype(key.dtype)

    def col_labels(j):
        return (vir_row[...] ^ occ_ref[kap * (depth // nvir) + j]).astype(jnp.float32).astype(wm.dtype)

    write_labels(rho, row_lab, row_key)

    def keep(key, labels, block):
        key = jnp.concatenate([key] * (nvir // key.shape[1]), axis=1)
        return jnp.where(key == labels, block, jnp.zeros_like(block))

    def mask(j):
        w_copy(j).wait()
        cols = pl.ds(pl.multiple_of(j * nvir, nvir), nvir)
        labels = col_labels(j)
        for b in range(nr // sub):
            block = wm[b * sub:(b + 1) * sub, cols]
            wm[b * sub:(b + 1) * sub, cols] = keep(row_key[b * sub:(b + 1) * sub, :], labels, block)

    if nh:
        def v_copy(g):
            return pltpu.make_async_remote_copy(
                src_ref=v_out.at[g], dst_ref=v_in.at[g],
                send_sem=v_send.at[g], recv_sem=v_recv.at[g],
                device_id=(patron, kap), device_id_type=MESH)

        def p_copy(p):
            at = pl.ds(2 * p, 2)
            return pltpu.make_async_remote_copy(
                src_ref=p_out.at[at], dst_ref=p_in.at[at],
                send_sem=p_send.at[p], recv_sem=p_recv.at[p],
                device_id=(helped, kap), device_id_type=MESH)

        @pl.when(is_end)
        def _():
            for b in range(nr // sub):
                mine = lane_labels(rho, b)
                rank = jnp.zeros((1, sub), jnp.float32)
                for c in range(b + 1):
                    same = row_lab[c * sub:(c + 1) * sub, :] == mine
                    if c == b:
                        same = same & (sub_i < lane_i)
                    rank = rank + jnp.sum(jnp.where(same, 1.0, 0.0), axis=0, keepdims=True)
                slot = lax.broadcasted_iota(jnp.int32, (cap, sub), 0).astype(jnp.float32)
                fold[:, b * sub:(b + 1) * sub] = jnp.where(slot == rank, 1.0, 0.0).astype(fold.dtype)

        @pl.when(helper)
        def _():
            p_acc[...] = jnp.zeros_like(p_acc)
            write_labels(helped, help_lab, help_key)
            for b in range(nr // sub):
                mine = help_lab[b * sub:(b + 1) * sub, :]
                rank = jnp.zeros((sub, 1), jnp.float32)
                for c in range(b + 1):
                    same = mine == lane_labels(helped, c)
                    if c == b:
                        same = same & (lane_i < sub_i)
                    rank = rank + jnp.sum(jnp.where(same, 1.0, 0.0), axis=1, keepdims=True)
                slot = lax.broadcasted_iota(jnp.int32, (sub, cap), 1).astype(jnp.float32)
                spread[b * sub:(b + 1) * sub, :] = jnp.where(slot == rank, 1.0, 0.0).astype(spread.dtype)

        def make_folded(g):
            def part(j):
                at = pl.ds(pl.multiple_of(j * nvir, nvir), nvir)
                cols = pl.ds(pl.multiple_of(g * kc + j * nvir, nvir), nvir)
                v = jnp.dot(fold[...], wm[:, cols], preferred_element_type=jnp.float32)
                v_out[g, :, at] = v.astype(v_out.dtype)

            loop(per_q, part)

        def v_ready(n):
            seen = counted(n, nh) - (nq - ahead + 2)
            ready = jnp.clip((seen + 2) // 2, 0, nh)
            return jnp.where(n <= nq, 0, jnp.where(n == (chips - 1) * nq, nh, ready))

        def help_with(g):
            v_copy(g).wait_recv()

            def part(j):
                at = pl.ds(pl.multiple_of(j * nvir, nvir), nvir)
                labels = col_labels(g * per_q + j)
                for b in range(nr // sub):
                    rows_b = slice(b * sub, (b + 1) * sub)
                    block = jnp.dot(spread[rows_b, :], v_in[g, :, at], preferred_element_type=jnp.float32)
                    w_help[rows_b, at] = keep(help_key[rows_b, :], labels, block.astype(w_help.dtype))

            loop(per_q, part)

            base = jnp.where(below, 2, 0)
            a = gath[pl.ds(base, nrow - 2), :, chunk(g)].reshape((nrow - 2) * rows, kc)
            p_acc[...] += lax.dot_general(w_help[...], a, NT, preferred_element_type=jnp.float32)

            @pl.when(g == nh - 1)
            def _():
                p_out[pl.ds(base, nrow - 2)] = p_acc[...].T.reshape(nrow - 2, rows, nr)
                loop(chips - 1, lambda t: p_copy(jnp.where(below, t + 1, t)).start())

    def product(p, q):
        a = gath[pl.ds(2 * p, 2), :, chunk(q)].reshape(2 * rows, kc)
        acc[p] += lax.dot_general(wm[:, chunk(q)], a, NT, preferred_element_type=jnp.float32)

    def finish(p, more=None):
        whole = acc[p].T.reshape(2, rows, nr)
        done[pl.ds(2 * p, 2)] = whole if more is None else whole + more[pl.ds(2 * p, 2)]
        send_done(p)

    def send_done(p):
        for e in range(2):
            s = 2 * p + e

            @pl.when(s // spo != kap)
            def _():
                reduce_copy(s).start()

    inner = has_up & has_down

    def product_near(q):
        base = 2 * (chip - 1)
        a = gath[pl.ds(base, 6), :, chunk(q)].reshape(6 * rows, kc)
        near[...] += lax.dot_general(wm[:, chunk(q)], a, NT, preferred_element_type=jnp.float32)

        @pl.when(q == nq - 1)
        def _():
            done[pl.ds(base, 6)] = near[...].T.reshape(6, rows, nr)
            loop(3, lambda t: send_done(chip - 1 + t))

    def own_step(q):
        loop(per_q, lambda j: mask(q * per_q + j))
        if nh:
            @pl.when(is_end & (q < nh))
            def _():
                make_folded(q)

        remote(2, other, q).wait_recv()

        @pl.when(jnp.logical_not(inner))
        def _():
            product(chip, q)

            @pl.when(q == nq - 1)
            def _():
                finish(chip)

    def source(way, i):
        d = i // nq + 1
        q = i % nq
        p = chip - d if way == 0 else chip + d
        there = p >= 0 if way == 0 else p < chips
        if nh:
            there = there & jnp.logical_not(is_end & (q < nh))
        return p, q, there

    def settle(t):
        p = jnp.where(first, t + 1, chips - 2 - t)
        at = pl.ds(2 * p, 2)
        pltpu.make_async_remote_copy(
            src_ref=p_out.at[at], dst_ref=p_in.at[at],
            send_sem=p_send.at[p], recv_sem=p_recv.at[p],
            device_id=(patron, kap), device_id_type=MESH).wait_recv()
        finish(p, p_in)

    def step(i):
        @pl.when(i < nq)
        def _():
            own_step(i)

        if nh:
            @pl.when(is_end & (i == (chips - 1) * nq - 1))
            def _():
                loop(chips - 2, settle)

        for way in range(2):
            p, q, there = source(way, i)

            @pl.when(there)
            def _():
                s = 2 * p + core
                remote(way, s, q).wait_recv()
                remote(2, s, q).start()

        for way in range(2):
            send_between(way, sendable(way, i), sendable(way, i + 1))

        if nh:
            @pl.when(is_end)
            def _():
                def send_v(g, c):
                    v_copy(g).start()
                    return c

                lax.fori_loop(v_ready(i), v_ready(i + 1), send_v, 0)

        for way in range(2):
            p, q, there = source(way, i)

            @pl.when(there)
            def _():
                remote(2, 2 * p + 1 - core, q).wait_recv()

                @pl.when(jnp.logical_not(inner & (i < nq)))
                def _():
                    product(p, q)

                    @pl.when((q == nq - 1) & jnp.logical_not(is_end) if nh else q == nq - 1)
                    def _():
                        finish(p)

        @pl.when(inner & (i < nq))
        def _():
            product_near(i)

        if nh:
            def maybe(g):
                ready = (chips - 3) * nq + (5 * (g + 1) + 1) // 2 - 1

                @pl.when(i == ready)
                def _():
                    help_with(g)

            @pl.when(helper)
            def _():
                loop(nh, maybe)

    loop((chips - 1) * nq, step)

    if nh:
        @pl.when(is_end)
        def _():
            settle(chips - 2)

    for i in range(spo):
        total = done[kap * spo + i]
        for t in range(1, ncol):
            peer = lax.rem(kap + t, ncol)
            pltpu.make_async_remote_copy(
                src_ref=done.at[i], dst_ref=red.at[peer, i],
                send_sem=rs_send.at[i], recv_sem=rs_recv.at[peer, i],
                device_id=(rho, peer), device_id_type=MESH).wait_recv()
            total = total + red[peer, i]
        out_ref[i * rows:(i + 1) * rows, :] = total

    def drain(i):
        p = i // nq
        q = i % nq
        s = 2 * p + core

        @pl.when(has_up & (p <= chip) & (q >= up_from))
        def _():
            remote(0, s, q).wait_send()

        @pl.when(has_down & (p >= chip) & (q >= down_from))
        def _():
            remote(1, s, q).wait_send()

        @pl.when((p == chip) | jnp.logical_not(is_end & (q < nh)) if nh else p >= 0)
        def _():
            remote(2, s, q).wait_send()

    loop(chips * nq, drain)

    if nh:
        @pl.when(is_end)
        def _():
            loop(nh, lambda g: v_copy(g).wait_send())

        @pl.when(helper)
        def _():
            loop(chips - 1, lambda t: p_copy(jnp.where(below, t + 1, t)).wait_send())

    def drain_reduce(s):
        @pl.when(s // spo != kap)
        def _():
            reduce_copy(s).wait_send()

    loop(nrow, drain_reduce)


def body(nrow, ncol, occ_irrep, vir_irrep, w_slab, amplitudes):
    rows, depth = amplitudes.shape
    nr = w_slab.shape[0]
    nvir = vir_irrep.shape[0]
    kc = KC if depth % KC == 0 else depth
    nq = depth // kc
    spo = nrow // ncol
    cap = -(-nr * 5 // 24 // 16) * 16
    help_chunks = 5 * nq // 16 if nrow // 2 >= 4 else 0
    vmem = pl.BlockSpec(memory_space=pltpu.VMEM)
    anywhere = pl.BlockSpec(memory_space=pl.ANY)

    def call(nh, *args):
        scratch = [
            pltpu.VMEM((nrow, rows, depth), amplitudes.dtype),
            pltpu.VMEM((nr, depth), w_slab.dtype),
            pltpu.VMEM((nrow // 2, nr, 2 * rows), jnp.float32),
            pltpu.VMEM((nr, 6 * rows), jnp.float32),
            pltpu.VMEM((nrow, rows, nr), jnp.float32),
            pltpu.VMEM((ncol, spo, rows, nr), jnp.float32),
            pltpu.VMEM((nr, 1), jnp.float32),
            pltpu.VMEM((nr, 128), w_slab.dtype),
            pltpu.SemaphoreType.DMA((depth // nvir,)),
            pltpu.SemaphoreType.DMA((nq,)),
            pltpu.SemaphoreType.DMA((3, nrow, nq)),
            pltpu.SemaphoreType.DMA((nrow, nq)),
            pltpu.SemaphoreType.DMA((nrow,)),
            pltpu.SemaphoreType.DMA((ncol, spo)),
        ]
        if nh:
            scratch += [
                pltpu.VMEM((nh, cap, kc), w_slab.dtype),
                pltpu.VMEM((nh, cap, kc), w_slab.dtype),
                pltpu.VMEM((nr, kc), w_slab.dtype),
                pltpu.VMEM((nr, (nrow - 2) * rows), jnp.float32),
                pltpu.VMEM((nrow, rows, nr), jnp.float32),
                pltpu.VMEM((nrow, rows, nr), jnp.float32),
                pltpu.VMEM((nr, 1), jnp.float32),
                pltpu.VMEM((nr, 128), w_slab.dtype),
                pltpu.VMEM((nr, cap), w_slab.dtype),
                pltpu.VMEM((cap, nr), w_slab.dtype),
                pltpu.SemaphoreType.DMA((nh,)),
                pltpu.SemaphoreType.DMA((nh,)),
                pltpu.SemaphoreType.DMA((nrow // 2,)),
                pltpu.SemaphoreType.DMA((nrow // 2,)),
            ]
        return pl.pallas_call(
            functools.partial(kernel, nrow, ncol, kc, nh, cap),
            out_shape=jax.ShapeDtypeStruct((spo * rows, nr), jnp.float32),
            in_specs=[pl.BlockSpec(memory_space=pltpu.SMEM), vmem, anywhere, anywhere],
            out_specs=vmem,
            scratch_shapes=scratch,
            compiler_params=pltpu.CompilerParams(
                collective_id=1 if nh else 0, has_side_effects=True, vmem_limit_bytes=58 * 1024 * 1024),
            cost_estimate=pl.CostEstimate(
                flops=2 * nrow * rows * nr * depth, bytes_accessed=2 * nr * depth, transcendentals=0),
        )(*args)

    args = (occ_irrep, vir_irrep.reshape(1, nvir), w_slab, amplitudes)
    if not help_chunks:
        return call(0, *args)
    nocc = -(-nrow * nr // nvir)
    labels = (occ_irrep[:nocc, None] ^ vir_irrep[None, :]).reshape(-1)[:nrow * nr].reshape(nrow, 1, nr)
    counts = jnp.sum(labels == jnp.arange(8, dtype=jnp.int32).reshape(1, 8, 1), axis=2)
    fits = jnp.max(counts) <= cap
    return lax.cond(fits, functools.partial(call, help_chunks), functools.partial(call, 0), *args)


def solution(mesh):
    placed = (P(), P(), P("row", "col"), P("row", "col"))
    shape = dict(mesh.shape)
    return jax.shard_map(
        functools.partial(body, shape["row"], shape["col"]), mesh=mesh,
        in_specs=placed, out_specs=P("col", "row"), check_vma=False)
```
